256 devices in a mesh: sec: 4 (over y), ctx: 16 (over z, x_hi), tp: 4 (over x_lo, core).
Axes of the slice: x: 4 (x_hi: 2, x_lo: 2; x = x_hi * 2 + x_lo), y: 4, z: 8, core: 2. Of those that a mesh axis runs over, the one named last changes fastest.
Arguments:
- self_query: bfloat16 [8192, 2048], P('ctx', ('sec', 'tp')), may hold values from -6 to 6
- self_key: bfloat16 [8192, 2048], P('ctx', ('sec', 'tp')), may hold values from -6 to 6
- self_value: bfloat16 [8192, 2048], P('ctx', ('sec', 'tp')), may hold values from -6 to 6
- self_gain: float32 [2048], P(('sec', 'tp')), may hold values from 0.5 to 1.5
- self_grad: bfloat16 [8192, 2048], P('ctx', ('sec', 'tp')), may hold values from -6 to 6
- cross_query: bfloat16 [8192, 2048], P('ctx', ('sec', 'tp')), may hold values from -6 to 6
- memory_key: bfloat16 [2048, 2048], P(('sec', 'ctx')), may hold values from -6 to 6
- memory_value: bfloat16 [2048, 2048], P(('sec', 'ctx')), may hold values from -6 to 6
- cross_gain: float32 [2048], P(('sec', 'tp')), may hold values from 0.5 to 1.5
- cross_grad: bfloat16 [8192, 2048], P('ctx', ('sec', 'tp')), may hold values from -6 to 6
- block_start: int32 [64], replicated, may hold values from 0 to 63, each once
Outputs:
- self_out: bfloat16 [8192, 2048], P('ctx', ('sec', 'tp'))
- cross_out: bfloat16 [8192, 2048], P('ctx', ('sec', 'tp'))
- query_grad: bfloat16 [8192, 2048], P('ctx', ('sec', 'tp'))
- key_grad: bfloat16 [8192, 2048], P('ctx', ('sec', 'tp'))
- value_grad: bfloat16 [8192, 2048], P('ctx', ('sec', 'tp'))
- cross_query_grad: bfloat16 [8192, 2048], P('ctx', ('sec', 'tp'))
- memory_key_grad: bfloat16 [2048, 2048], P(('sec', 'ctx'))
- memory_value_grad: bfloat16 [2048, 2048], P(('sec', 'ctx'))
The draws below stay inside these ranges and needn't reach their ends.
Inputs may be any that keep to these rules, and one draw needn't show every extreme that they name: `block_start`: every number appears once.
All inputs are finite; a program needn't handle non-finite values.
Results may differ from the reference program's by a relative error of at most 0.015.
Values may be sent and summed in bfloat16 or wider, within the bound.
A program may use at most 64 MiB of HBM per device.

```python
import math
import jax
import jax.numpy as jnp
from jax import lax

HEADS = 16
HEAD_DIM = 128
FR_DEV = 512
FRAMES = 8192
MEMORY = 2048
N_CTX = 16


def base_draw(key, row_count):
    return jnp.clip(jax.random.normal(key, (row_count, HEADS * HEAD_DIM), jnp.float32), -6.0, 6.0)


def head_scales():
    head_ids = jnp.arange(HEADS * HEAD_DIM) // HEAD_DIM
    position_ratio = head_ids.astype(jnp.float32) / max(HEADS - 1, 1)
    return 3.0 ** position_ratio / 1.7


def value_draw(key, row_count):
    base_values = jax.random.normal(key, (row_count, HEADS * HEAD_DIM), jnp.float32)
    return jnp.clip(base_values * head_scales()[None, :], -6.0, 6.0)


def draw_self_query(key, part):
    drawn = base_draw(jax.random.fold_in(key, 101), FRAMES)
    return drawn.astype(jnp.bfloat16)


def draw_self_key(key, part):
    drawn = base_draw(jax.random.fold_in(key, 102), FRAMES)
    return drawn.astype(jnp.bfloat16)


def draw_self_value(key, part):
    return value_draw(jax.random.fold_in(key, 103), FRAMES).astype(jnp.bfloat16)


def draw_cross_query(key, part):
    drawn = base_draw(jax.random.fold_in(key, 104), FRAMES)
    return drawn.astype(jnp.bfloat16)


def draw_memory_key(key, part):
    drawn = base_draw(jax.random.fold_in(key, 105), MEMORY)
    return drawn.astype(jnp.bfloat16)


def draw_memory_value(key, part):
    return value_draw(jax.random.fold_in(key, 106), MEMORY).astype(jnp.bfloat16)


def steps_of(stream_key, shape, shards, least, top_value):
    level, own = 1.0, jax.random.fold_in(stream_key, 6)
    for axis_at, parts in shards:
        heights = jnp.exp(jax.random.uniform(jax.random.fold_in(own, axis_at), (parts,), jnp.float32, least / len(shards), top_value / len(shards)))
        level = level * jnp.repeat(heights, shape[axis_at] // parts).reshape([-1 if axis == axis_at else 1 for axis in range(len(shape))])
    return level


def noise(stream_key, shape, width, bound, pieces=(), kind=jnp.bfloat16):
    level = steps_of(stream_key, shape, pieces, -0.22, 0.18) if pieces else 1.0
    values = jax.random.normal(stream_key, shape, jnp.float32) * width * level
    return jnp.minimum(jnp.maximum(values, -bound), bound).astype(kind)


def setup_inputs(seed: int = 0) -> dict:
    splits = jax.random.split(jax.random.key(seed), 12)
    self_query = draw_self_query(jax.random.fold_in(splits[11], 71), 0)
    self_key = draw_self_key(jax.random.fold_in(splits[11], 71), 0)
    self_value = draw_self_value(jax.random.fold_in(splits[11], 71), 0)
    self_gain = jnp.clip(1.0 + 0.1 * jax.random.normal(splits[3], (HEADS * HEAD_DIM,), jnp.float32), 0.5, 1.5)
    self_grad = noise(splits[4], (FRAMES, HEADS * HEAD_DIM), 1.0, 6.0, ((0, 16), (1, 16)))
    cross_query = draw_cross_query(jax.random.fold_in(splits[11], 71), 0)
    memory_key = draw_memory_key(jax.random.fold_in(splits[11], 71), 0)
    memory_value = draw_memory_value(jax.random.fold_in(splits[11], 71), 0)
    cross_gain = jnp.clip(1.0 + 0.1 * jax.random.normal(splits[8], (HEADS * HEAD_DIM,), jnp.float32), 0.5, 1.5)
    cross_grad = noise(splits[9], (FRAMES, HEADS * HEAD_DIM), 1.0, 6.0, ((0, 16), (1, 16)))
    block_start = jax.random.permutation(splits[10], 4 * N_CTX).astype(jnp.int32)
    return dict(self_query=self_query, self_key=self_key, self_value=self_value, self_gain=self_gain, self_grad=self_grad, cross_query=cross_query, memory_key=memory_key, memory_value=memory_value, cross_gain=cross_gain, cross_grad=cross_grad, block_start=block_start)


EPS = 1e-06

def heads_first(matrix):
    return matrix.reshape(matrix.shape[0], HEADS, HEAD_DIM).transpose(1, 0, 2)

def heads_last(stacked):
    return stacked.transpose(1, 0, 2).reshape(stacked.shape[1], HEADS * HEAD_DIM)

def in_blocks(tensor_in, block_rows):
    return tensor_in.reshape((tensor_in.shape[0] // block_rows, block_rows) + tensor_in.shape[1:])

def head_scores(queries, key_rows, query_position, key_position, causal):
    scores = jnp.dot(queries, key_rows.T, preferred_element_type=jnp.float32) * (1.0 / math.sqrt(HEAD_DIM))
    if causal:
        scores = jnp.where(key_position[None, :] > query_position[:, None], -jnp.inf, scores)
    return scores

def forward_head(queries, key_rows, value_rows, query_position, key_position, causal, block_rows):

    def one_block(packed):
        block_queries, block_position = packed
        scores = head_scores(block_queries, key_rows, block_position, key_position, causal)
        row_top = lax.optimization_barrier(jnp.max(scores, axis=1))
        log_total = row_top + jnp.log(lax.optimization_barrier(jnp.sum(jnp.exp(scores - row_top[:, None]), axis=1)))
        weights = jnp.exp(scores - log_total[:, None]).astype(jnp.bfloat16)
        return (log_total, jnp.dot(weights, value_rows, preferred_element_type=jnp.float32))
    log_total, attended = lax.map(one_block, (in_blocks(queries, block_rows), in_blocks(query_position, block_rows)))
    return (log_total.reshape(-1), attended.reshape(-1, HEAD_DIM))

def backward_head(queries, key_rows, value_rows, cotangent, attended, log_total, query_position, key_position, causal, block_rows):
    row_delta = lax.optimization_barrier(jnp.sum(cotangent.astype(jnp.float32) * attended, axis=1))
    scaling = 1.0 / math.sqrt(HEAD_DIM)

    def one_block(carried, packed):
        key_sum, value_sum = carried
        block_queries, block_grad, block_total, block_delta, block_position = packed
        scores = head_scores(block_queries, key_rows, block_position, key_position, causal)
        weights = jnp.exp(scores - block_total[:, None])
        products = jnp.dot(block_grad, value_rows.T, preferred_element_type=jnp.float32)
        score_grad = (weights * (products - block_delta[:, None])).astype(jnp.bfloat16)
        query_part = jnp.dot(score_grad, key_rows, preferred_element_type=jnp.float32) * scaling
        key_sum = key_sum + jnp.dot(score_grad.T, block_queries, preferred_element_type=jnp.float32) * scaling
        value_sum = value_sum + jnp.dot(weights.astype(jnp.bfloat16).T, block_grad, preferred_element_type=jnp.float32)
        return ((key_sum, value_sum), query_part)
    zeros = jnp.zeros(key_rows.shape, jnp.float32)
    packed = (in_blocks(queries, block_rows), in_blocks(cotangent, block_rows), in_blocks(log_total, block_rows), in_blocks(row_delta, block_rows), in_blocks(query_position, block_rows))
    (key_sum, value_sum), query_part = lax.scan(one_block, (zeros, zeros), packed)
    return (query_part.reshape(-1, HEAD_DIM), key_sum, value_sum)

def attention_part(queries, key_rows, value_rows, gain, cotangent, query_position, key_position, causal):
    block_rows = math.gcd(FRAMES, 1024)
    query_heads = heads_first(queries)
    key_heads = heads_first(key_rows)
    value_heads = heads_first(value_rows)

    def forward_one(packed):
        return forward_head(packed[0], packed[1], packed[2], query_position, key_position, causal, block_rows)
    log_total, attended = lax.map(forward_one, (query_heads, key_heads, value_heads))
    flattened = heads_last(attended)
    row_scale = lax.rsqrt(lax.optimization_barrier(jnp.mean(flattened * flattened, axis=1)) + EPS)
    output = (gain[None, :] * flattened * row_scale[:, None]).astype(jnp.bfloat16)
    lifted = gain[None, :] * cotangent.astype(jnp.float32)
    row_slope = lax.optimization_barrier(jnp.mean(lifted * flattened, axis=1))
    attended_grad = (row_scale[:, None] * (lifted - flattened * (row_scale * row_scale * row_slope)[:, None])).astype(jnp.bfloat16)
    grad_heads = heads_first(attended_grad)

    def backward_one(packed):
        return backward_head(packed[0], packed[1], packed[2], packed[3], packed[4], packed[5], query_position, key_position, causal, block_rows)
    query_part, key_part, value_part = lax.map(backward_one, (query_heads, key_heads, value_heads, grad_heads, attended, log_total))
    return (output, heads_last(query_part).astype(jnp.bfloat16), heads_last(key_part).astype(jnp.bfloat16), heads_last(value_part).astype(jnp.bfloat16))

def reference(self_query, self_key, self_value, self_gain, self_grad, cross_query, memory_key, memory_value, cross_gain, cross_grad, block_start):
    quarter = FR_DEV // 4
    row_ids = jnp.arange(FRAMES, dtype=jnp.int32)
    position = (block_start[row_ids // quarter] * quarter + row_ids % quarter).astype(jnp.int32)
    memory_position = jnp.zeros((MEMORY,), jnp.int32)
    self_out, query_grad, key_grad, value_grad = attention_part(self_query, self_key, self_value, self_gain, self_grad, position, position, True)
    cross_out, cross_query_grad, memory_key_grad, memory_value_grad = attention_part(cross_query, memory_key, memory_value, cross_gain, cross_grad, position, memory_position, False)
    return (self_out, cross_out, query_grad, key_grad, value_grad, cross_query_grad, memory_key_grad, memory_value_grad)
```

```python
import functools
import math

import jax
import jax.numpy as jnp
from jax import lax
from jax.experimental import pallas as pl
from jax.experimental.pallas import tpu as pltpu
from jax.sharding import PartitionSpec as P

HEAD_DIM = 128
EPS = 1e-06
NEG = -1e30
SCALE = 1.0 / math.sqrt(HEAD_DIM)
C2 = SCALE * math.log2(math.e)
TQ = 256
MESH = pl.DeviceIdType.MESH
F32 = jnp.float32
BF16 = jnp.bfloat16
SELF, CROSS = 0, 1


def dot(a, b, ca, cb):
    return lax.dot_general(a, b, (((ca,), (cb,)), ((), ())), preferred_element_type=F32)


def pack_rows(ref, vectors):
    row = 0
    for v in vectors:
        for i in range(v.shape[1] // 128):
            ref[row : row + 1, :] = v[:, i * 128 : (i + 1) * 128]
            row += 1


def unpack_rows(tile, row, count):
    return jnp.concatenate([tile[row + i : row + i + 1, :] for i in range(count)], axis=1)


def kernel(
    nz, nsec, ntp, n_sems,
    bs, q_in, k_in, v_in, sgain, sgrad, cq_in, mk_in, mv_in, cgain, cgrad,
    self_out, cross_out, query_grad, key_grad, value_grad, cross_query_grad, mkey_grad, mvalue_grad,
    kv, qs, mb, acc, ml, ot, lifted, osend, orecv, ostat, ostat_r, nsend, nrecv, do, dstat,
    dq, dqs, dqr, kacc, rs_s, rs_r, ms, mrs_s, mrs_r, mfin, mout,
    ssem, rsem, lsem,
):
    rows = q_in.shape[0]
    mrows = mk_in.shape[0]
    srows = nsec * mrows
    half = nz // 2
    full = nsec * ntp * HEAD_DIM
    nt = rows // TQ
    nsub = rows // 128

    sec, ctx, tp = lax.axis_index("sec"), lax.axis_index("ctx"), lax.axis_index("tp")
    z, x = ctx // 2, ctx % 2
    head = sec * ntp + tp

    def dev(zz, xx):
        return (sec, zz * 2 + xx, tp)

    right = dev(lax.rem(z + 1, nz), x)
    left = dev(lax.rem(z + nz - 1, nz), x)
    partner = dev(z, 1 - x)

    def peer(o):
        return (lax.rem(sec + o // ntp, nsec), ctx, lax.rem(tp + o % ntp, ntp))

    n_peers = nsec * ntp

    count = [0]

    def sem_id():
        count[0] += 1
        assert count[0] <= n_sems
        return count[0] - 1

    sent = []

    def copy(src, dst, i, to):
        return pltpu.make_async_remote_copy(
            src_ref=src, dst_ref=dst, send_sem=ssem.at[i], recv_sem=rsem.at[i], device_id=to, device_id_type=MESH
        )

    def send(src, dst, i, to):
        c = copy(src, dst, i, to)
        c.start()
        sent.append(c)

    def arrive(dst, i, frm):
        copy(dst, dst, i, frm).wait_recv()

    local = [
        pltpu.make_async_copy(k_in, kv.at[z, 0], lsem.at[0]),
        pltpu.make_async_copy(v_in, kv.at[z, 1], lsem.at[1]),
        pltpu.make_async_copy(q_in, qs.at[SELF, x], lsem.at[2]),
        pltpu.make_async_copy(cq_in, qs.at[CROSS, x], lsem.at[3]),
    ]
    own_cols = pl.ds(pl.multiple_of(head * HEAD_DIM, HEAD_DIM), HEAD_DIM)
    own_rows = pl.ds(pl.multiple_of(sec * mrows, mrows), mrows)
    local += [
        pltpu.make_async_copy(mk_in.at[:, own_cols], mb.at[z, 0, own_rows, :], lsem.at[4]),
        pltpu.make_async_copy(mv_in.at[:, own_cols], mb.at[z, 1, own_rows, :], lsem.at[5]),
    ]
    for c in local:
        c.start()

    barrier = pltpu.get_barrier_semaphore()
    everyone = [right, left, partner] + [peer(o) for o in range(1, n_peers)]
    for to in everyone:
        pl.semaphore_signal(barrier, inc=1, device_id=to, device_id_type=MESH)
    pl.semaphore_wait(barrier, len(everyone))

    mem_ids = []
    for o in range(1, nsec):
        to = (lax.rem(sec + o, nsec), ctx, tp)
        cols = pl.ds(pl.multiple_of((lax.rem(sec + o, nsec) * ntp + tp) * HEAD_DIM, HEAD_DIM), HEAD_DIM)
        for j, src in enumerate((mk_in, mv_in)):
            i = sem_id()
            send(src.at[:, cols], mb.at[z, j, own_rows, :], i, to)
            mem_ids.append((o, j, i))

    def zoff(d):
        return lax.rem(z + nz + d, nz)

    def ring_ids():
        return [(sem_id(), sem_id()) for _ in range(half)]

    kv_ids, mb_ids = ring_ids(), ring_ids()

    def ring_send(buf, ids, s):
        r, l = ids[s - 1]
        a, b = zoff(-(s - 1)), zoff(s - 1)
        if s < half:
            send(buf.at[a], buf.at[a], r, right)
            send(buf.at[b], buf.at[b], l, left)
        else:
            send(buf.at[a, 0], buf.at[a, 0], r, right)
            send(buf.at[b, 1], buf.at[b, 1], l, left)

    def ring_arrive(buf, ids, s):
        r, l = ids[s - 1]
        a, b = zoff(-s), zoff(s)
        if s < half:
            arrive(buf.at[a], r, left)
            arrive(buf.at[b], l, right)
        else:
            arrive(buf.at[a, 0], r, left)
            arrive(buf.at[b, 1], l, right)

    local[0].wait()
    local[1].wait()
    ring_send(kv, kv_ids, 1)
    q_ids = [sem_id(), sem_id()]
    for a in (SELF, CROSS):
        local[2 + a].wait()
        send(qs.at[a, x], qs.at[a, x], q_ids[a], partner)

    acc[...] = jnp.zeros_like(acc)
    dq[...] = jnp.zeros_like(dq)
    for a in (SELF, CROSS):
        for h in range(2):
            ml[a, h, 0:1, :] = jnp.full((1, rows), NEG, F32)
            ml[a, h, 1:2, :] = jnp.zeros((1, rows), F32)
    for a, (gain, grad) in enumerate(((sgain, sgrad), (cgain, cgrad))):
        lifted[a] = (gain[...] * grad[...].astype(F32)).T

    def query_positions(h, t):
        lane = lax.broadcasted_iota(jnp.int32, (1, 128), 1)
        first = (z * 2 + h) * nsub + t * (TQ // 128)
        return jnp.concatenate([bs[first + i] * 128 + lane for i in range(TQ // 128)], axis=1)

    def masked(s, slot, h, t):
        qpos = query_positions(h, t)
        first = (slot * 2 + x) * nsub
        row = lax.broadcasted_iota(jnp.int32, (128, TQ), 0)
        out = []
        for kb in range(nsub):
            gone = row > qpos - bs[first + kb] * 128
            out.append(jnp.where(gone, NEG, s[kb * 128 : (kb + 1) * 128, :]))
        return jnp.concatenate(out, axis=0)

    def forward(a, h, keys, values_t, slot):
        for t in range(nt):
            cols = slice(t * TQ, (t + 1) * TQ)
            s = dot(keys, qs[a, h, cols, :], 1, 1)
            if slot is not None:
                s = masked(s, slot, h, t)
            old = ml[a, h, 0:1, cols]
            new = jnp.maximum(old, jnp.max(s, axis=0, keepdims=True))
            p = jnp.exp2((s - new) * C2)
            shrink = jnp.exp2((old - new) * C2)
            ml[a, h, 0:1, cols] = new
            ml[a, h, 1:2, cols] = ml[a, h, 1:2, cols] * shrink + jnp.sum(p, axis=0, keepdims=True)
            acc[a, h, :, cols] = acc[a, h, :, cols] * shrink + dot(values_t, p.astype(BF16), 1, 0)

    def self_forward(slot, h):
        forward(SELF, h, kv[slot, 0], kv[slot, 1].T, slot)

    def cross_group(g, j):
        per = rows // srows
        return mb[pl.ds(g * per, per), j].reshape(rows, HEAD_DIM)

    n_groups = nz * srows // rows

    def cross_forward():
        def one(i, c):
            g, h = i // 2, i % 2
            forward(CROSS, h, cross_group(g, 0), cross_group(g, 1).T, None)
            return c

        lax.fori_loop(0, n_groups * 2, one, 0)

    self_forward(z, x)
    local[4].wait()
    local[5].wait()
    for o, j, i in mem_ids:
        frm = lax.rem(sec + nsec - o, nsec)
        dst = mb.at[z, j, pl.ds(pl.multiple_of(frm * mrows, mrows), mrows), :]
        arrive(dst, i, (frm, ctx, tp))
    ring_send(mb, mb_ids, 1)
    for a in (SELF, CROSS):
        arrive(qs.at[a, 1 - x], q_ids[a], partner)
    self_forward(z, 1 - x)
    for s in range(1, half):
        ring_arrive(kv, kv_ids, s)
        ring_send(kv, kv_ids, s + 1)
        ring_arrive(mb, mb_ids, s)
        ring_send(mb, mb_ids, s + 1)

        def pair(i, c, s=s):
            self_forward(zoff((2 * (i // 2) - 1) * s), i % 2)
            return c

        lax.fori_loop(0, 4, pair, 0)
    ring_arrive(kv, kv_ids, half)
    ring_arrive(mb, mb_ids, half)

    def last(i, c):
        self_forward(zoff(half), i)
        return c

    lax.fori_loop(0, 2, last, 0)

    o_ids = [(sem_id(), sem_id()) for _ in range(2)]
    n_ids = [[sem_id() for _ in range(1, n_peers)] for _ in range(2)]
    do_ids = [(sem_id(), sem_id()) for _ in range(2)]
    dq_ids = [sem_id(), sem_id()]

    def normed(a, h):
        total = ml[a, h, 1:2, :]
        return acc[a, h] * (1.0 / total), ml[a, h, 0:1, :] * C2 + jnp.log2(total)

    def send_partial(a):
        o, lse = normed(a, 1 - x)
        osend[a] = o.astype(BF16)
        pack_rows(ostat.at[a], [lse])
        send(osend.at[a], orecv.at[a], o_ids[a][0], partner)
        send(ostat.at[a], ostat_r.at[a], o_ids[a][1], partner)

    def combine(a):
        o0, l0 = normed(a, x)
        arrive(orecv.at[a], o_ids[a][0], partner)
        arrive(ostat_r.at[a], o_ids[a][1], partner)
        l1 = unpack_rows(ostat_r[a], 0, nsub)
        top = jnp.maximum(l0, l1)
        w0, w1 = jnp.exp2(l0 - top), jnp.exp2(l1 - top)
        total = w0 + w1
        inv = 1.0 / total
        o = o0 * (w0 * inv) + orecv[a].astype(F32) * (w1 * inv)
        ot[a] = o
        lse = top + jnp.log2(total)
        pack_rows(dstat.at[a, x], [lse])
        pack_rows(
            nsend.at[a],
            [jnp.sum(o * o, axis=0, keepdims=True), jnp.sum(lifted[a] * o, axis=0, keepdims=True)],
        )
        for k in range(1, n_peers):
            send(nsend.at[a], nrecv.at[a, k - 1], n_ids[a][k - 1], peer(k))

    def norm(a, gain, out):
        total = nsend[a]
        for k in range(1, n_peers):
            o = n_peers - k
            frm = (lax.rem(sec + nsec - k // ntp, nsec), ctx, lax.rem(tp + ntp - k % ntp, ntp))
            arrive(nrecv.at[a, k - 1], n_ids[a][k - 1], frm)
            total = total + nrecv[a, k - 1]
        scale = lax.rsqrt(unpack_rows(total, 0, nsub) / full + EPS)
        slope = unpack_rows(total, nsub, nsub) / full
        o = ot[a]
        g = (scale * (lifted[a] - o * (scale * scale * slope))).astype(BF16)
        do[a, x] = g
        delta = jnp.sum(g.astype(F32) * o, axis=0, keepdims=True)
        pack_rows(dstat.at[a, x, nsub : 2 * nsub], [delta])
        send(do.at[a, x], do.at[a, x], do_ids[a][0], partner)
        send(dstat.at[a, x], dstat.at[a, x], do_ids[a][1], partner)
        out[...] = (gain[...] * (o * scale).T).astype(BF16)

    send_partial(SELF)
    cross_forward()
    send_partial(CROSS)
    combine(SELF)
    combine(CROSS)
    norm(SELF, sgain, self_out)
    norm(CROSS, cgain, cross_out)

    def backward(a, h, keys, values, keys_t, slot, into):
        dk = dv = None
        for t in range(nt):
            cols = slice(t * TQ, (t + 1) * TQ)
            q = qs[a, h, cols, :]
            g = do[a, h, :, cols]
            stat = dstat[a, h]
            lse = unpack_rows(stat, t * (TQ // 128), TQ // 128)
            delta = unpack_rows(stat, nsub + t * (TQ // 128), TQ // 128)
            s = dot(keys, q, 1, 1)
            if slot is not None:
                s = masked(s, slot, h, t)
            p = jnp.exp2(s * C2 - lse)
            ds = (p * (dot(values, g, 1, 0) - delta)).astype(BF16)
            dv_t = dot(p.astype(BF16), g, 1, 1)
            dk_t = dot(ds, q, 1, 0)
            dv = dv_t if dv is None else dv + dv_t
            dk = dk_t if dk is None else dk + dk_t
            dq[a, h, :, cols] = dq[a, h, :, cols] + dot(keys_t, ds, 1, 0)
        kacc[into, 0] = kacc[into, 0] + dk * SCALE
        kacc[into, 1] = kacc[into, 1] + dv

    def self_backward(slot, h, into):
        backward(SELF, h, kv[slot, 0], kv[slot, 1], kv[slot, 0].T, slot, into)

    rs_ids = ring_ids()
    mrs_ids = ring_ids()

    def reduce_step(s, part, recv, snd, ids):
        r, l = ids[s - 1]
        if s == 1:
            snd[0, 0, 0] = part(0, 0).astype(BF16)
            snd[1, 0, 1] = part(1, 1).astype(BF16)
            send(snd.at[0, 0, 0], recv.at[0, 0, 0], r, right)
            send(snd.at[1, 0, 1], recv.at[1, 0, 1], l, left)
            return
        reduce_arrive(s - 1, recv, ids)
        for d in range(2):
            for j in range(2):
                own = part(d, j)
                if s > 2 or j == d:
                    own = own + recv[d, s - 2, j].astype(F32)
                snd[d, s - 1, j] = own.astype(BF16)
        send(snd.at[0, s - 1], recv.at[0, s - 1], r, right)
        send(snd.at[1, s - 1], recv.at[1, s - 1], l, left)

    def reduce_arrive(s, recv, ids):
        r, l = ids[s - 1]
        if s == 1:
            arrive(recv.at[0, 0, 0], r, left)
            arrive(recv.at[1, 0, 1], l, right)
        else:
            arrive(recv.at[0, s - 1], r, left)
            arrive(recv.at[1, s - 1], l, right)

    def do_arrive(a):
        arrive(do.at[a, 1 - x], do_ids[a][0], partner)
        arrive(dstat.at[a, 1 - x], do_ids[a][1], partner)

    def cross_backward():
        per = rows // srows

        def one(g, c):
            kacc[0] = jnp.zeros_like(kacc[0])
            keys, values = cross_group(g, 0), cross_group(g, 1)
            keys_t = keys.T

            def each(h, c2):
                backward(CROSS, h, cross_group(g, 0), cross_group(g, 1), keys_t, None, 0)
                return c2

            lax.fori_loop(0, 2, each, 0)
            for j in range(2):
                ms[pl.ds(g * per, per), j] = kacc[0, j].reshape(per, srows, HEAD_DIM)
            return c

        lax.fori_loop(0, n_groups, one, 0)

    def mem_part(s):
        return lambda d, j: ms[zoff((1 - 2 * d) * (half + 1 - s)), j]

    kacc[0] = jnp.zeros_like(kacc[0])
    self_backward(zoff(half), x, 0)
    do_arrive(SELF)
    self_backward(zoff(half), 1 - x, 0)
    reduce_step(1, lambda d, j: kacc[0, j], rs_r, rs_s, rs_ids)
    for s in range(2, half + 1):
        dist = half + 1 - s
        kacc[...] = jnp.zeros_like(kacc)

        def back_pair(i, c, dist=dist):
            d, h = i // 2, i % 2
            self_backward(zoff((1 - 2 * d) * dist), h, d)
            return c

        lax.fori_loop(0, 4, back_pair, 0)
        reduce_step(s, lambda d, j: kacc[d, j], rs_r, rs_s, rs_ids)
        if s == 2:
            do_arrive(CROSS)
            cross_backward()
            dqs[CROSS] = dq[CROSS, 1 - x].astype(BF16)
            send(dqs.at[CROSS], dqr.at[CROSS], dq_ids[CROSS], partner)
            reduce_step(1, mem_part(1), mrs_r, mrs_s, mrs_ids)
        else:
            reduce_step(s - 1, mem_part(s - 1), mrs_r, mrs_s, mrs_ids)
    kacc[0] = jnp.zeros_like(kacc[0])

    def back_own(h, c):
        self_backward(z, h, 0)
        return c

    lax.fori_loop(0, 2, back_own, 0)
    dqs[SELF] = dq[SELF, 1 - x].astype(BF16)
    send(dqs.at[SELF], dqr.at[SELF], dq_ids[SELF], partner)
    reduce_step(half, mem_part(half), mrs_r, mrs_s, mrs_ids)

    def reduced(own, recv, j):
        return (own + recv[0, half - 1, j].astype(F32) + recv[1, half - 1, j].astype(F32)).astype(BF16)

    def finish_query(a, out):
        arrive(dqr.at[a], dq_ids[a], partner)
        out[...] = ((dq[a, x] + dqr[a].astype(F32)) * SCALE).T.astype(BF16)

    finish_query(CROSS, cross_query_grad)
    reduce_arrive(half, rs_r, rs_ids)
    key_grad[...] = reduced(kacc[0, 0], rs_r, 0)
    value_grad[...] = reduced(kacc[0, 1], rs_r, 1)
    reduce_arrive(half, mrs_r, mrs_ids)
    for j in range(2):
        mfin[j] = reduced(ms[z, j], mrs_r, j)
    ret_ids = [sem_id() for _ in range(1, n_peers)]
    for k in range(1, n_peers):
        to = peer(k)
        src_rows = pl.ds(pl.multiple_of(to[0] * mrows, mrows), mrows)
        send(mfin.at[:, src_rows, :], mout.at[:, :, own_cols], ret_ids[k - 1], to)
    mine = pltpu.make_async_copy(mfin.at[:, own_rows, :], mout.at[:, :, own_cols], lsem.at[0])
    mine.start()
    finish_query(SELF, query_grad)
    mine.wait()
    for k in range(1, n_peers):
        fs, ft = lax.rem(sec + nsec - k // ntp, nsec), lax.rem(tp + ntp - k % ntp, ntp)
        cols = pl.ds(pl.multiple_of((fs * ntp + ft) * HEAD_DIM, HEAD_DIM), HEAD_DIM)
        arrive(mout.at[:, :, cols], ret_ids[k - 1], (fs, ctx, ft))
    mkey_grad[...] = mout[0]
    mvalue_grad[...] = mout[1]
    for c in sent:
        c.wait_send()


def per_device(nz, nsec, ntp, *args):
    (sq, sk, sv, sgain, sgrad, cq, mk, mv, cgain, cgrad, bs) = args
    rows = sq.shape[0]
    mrows = mk.shape[0]
    half = nz // 2
    srows = nsec * mrows
    n_sems = 160
    any_spec = pl.BlockSpec(memory_space=pl.ANY)
    vmem = pl.BlockSpec(memory_space=pltpu.VMEM)
    smem = pl.BlockSpec(memory_space=pltpu.SMEM)
    frame = jax.ShapeDtypeStruct((rows, HEAD_DIM), BF16)
    memory = jax.ShapeDtypeStruct(mk.shape, BF16)
    V = pltpu.VMEM
    return pl.pallas_call(
        functools.partial(kernel, nz, nsec, ntp, n_sems),
        out_shape=(frame, frame, frame, frame, frame, frame, memory, memory),
        in_specs=[smem, any_spec, any_spec, any_spec, vmem, vmem, any_spec, any_spec, any_spec, vmem, vmem],
        out_specs=(vmem,) * 8,
        scratch_shapes=[
            V((nz, 2, rows, HEAD_DIM), BF16),
            V((2, 2, rows, HEAD_DIM), BF16),
            V((nz, 2, srows, HEAD_DIM), BF16),
            V((2, 2, HEAD_DIM, rows), F32),
            V((2, 2, 8, rows), F32),
            V((2, HEAD_DIM, rows), F32),
            V((2, HEAD_DIM, rows), F32),
            V((2, HEAD_DIM, rows), BF16),
            V((2, HEAD_DIM, rows), BF16),
            V((2, 8, 128), F32),
            V((2, 8, 128), F32),
            V((2, 8, 128), F32),
            V((2, nsec * ntp, 8, 128), F32),
            V((2, 2, HEAD_DIM, rows), BF16),
            V((2, 2, 8, 128), F32),
            V((2, 2, HEAD_DIM, rows), F32),
            V((2, HEAD_DIM, rows), BF16),
            V((2, HEAD_DIM, rows), BF16),
            V((2, 2, rows, HEAD_DIM), F32),
            V((2, half, 2, rows, HEAD_DIM), BF16),
            V((2, half, 2, rows, HEAD_DIM), BF16),
            V((nz, 2, srows, HEAD_DIM), F32),
            V((2, half, 2, srows, HEAD_DIM), BF16),
            V((2, half, 2, srows, HEAD_DIM), BF16),
            V((2, srows, HEAD_DIM), BF16),
            V((2, mrows, nsec * ntp * HEAD_DIM), BF16),
            pltpu.SemaphoreType.DMA((n_sems,)),
            pltpu.SemaphoreType.DMA((n_sems,)),
            pltpu.SemaphoreType.DMA((8,)),
        ],
        compiler_params=pltpu.CompilerParams(
            collective_id=0, has_side_effects=True, vmem_limit_bytes=48 * 1024 * 1024
        ),
        cost_estimate=pl.CostEstimate(flops=9_000_000_000, bytes_accessed=4_000_000, transcendentals=10_000_000),
    )(bs, sq, sk, sv, sgain.reshape(1, -1), sgrad, cq, mk, mv, cgain.reshape(1, -1), cgrad)


def solution(mesh):
    nz, nsec, ntp = mesh.shape["ctx"] // 2, mesh.shape["sec"], mesh.shape["tp"]
    heads = ("sec", "tp")
    frame, gain, memory = P("ctx", heads), P(heads), P(("sec", "ctx"), None)
    return jax.shard_map(
        functools.partial(per_device, nz, nsec, ntp),
        mesh=mesh,
        in_specs=(frame, frame, frame, gain, frame, frame, memory, memory, gain, frame, P()),
        out_specs=(frame,) * 6 + (memory,) * 2,
        check_vma=False,
    )
```

```python
import functools
import math

import jax
import jax.numpy as jnp
from jax import lax
from jax.experimental import pallas as pl
from jax.experimental.pallas import tpu as pltpu
from jax.sharding import PartitionSpec as P

HEAD_DIM = 128
EPS = 1e-06
NEG = -1e30
SCALE = 1.0 / math.sqrt(HEAD_DIM)
C2 = SCALE * math.log2(math.e)
TQ = 256
MESH = pl.DeviceIdType.MESH
F32 = jnp.float32
BF16 = jnp.bfloat16
SELF, CROSS = 0, 1


def dot(a, b, ca, cb):
    return lax.dot_general(a, b, (((ca,), (cb,)), ((), ())), preferred_element_type=F32)


def pack_rows(ref, vectors):
    row = 0
    for v in vectors:
        for i in range(v.shape[1] // 128):
            ref[row : row + 1, :] = v[:, i * 128 : (i + 1) * 128]
            row += 1


def unpack_rows(tile, row, count):
    return jnp.concatenate([tile[row + i : row + i + 1, :] for i in range(count)], axis=1)


def kernel(
    nz, nsec, ntp, n_sems,
    bs, q_in, k_in, v_in, sgain, sgrad, cq_in, mk_in, mv_in, cgain, cgrad,
    self_out, cross_out, query_grad, key_grad, value_grad, cross_query_grad, mkey_grad, mvalue_grad,
    kv, qs, mb, acc, ml, ot, lifted, osend, orecv, ostat, ostat_r, nsend, nrecv, do, dstat,
    dq, dqs, dqr, kacc, rs_s, rs_r, ms, mrs_s, mrs_r, mfin, mout,
    grads, gains,
    ssem, rsem, lsem,
):
    rows = q_in.shape[0]
    mrows = mk_in.shape[0]
    srows = nsec * mrows
    half = nz // 2
    full = nsec * ntp * HEAD_DIM
    nsub = rows // 128

    sec, ctx, tp = lax.axis_index("sec"), lax.axis_index("ctx"), lax.axis_index("tp")
    z, x = ctx // 2, ctx % 2
    head = sec * ntp + tp

    def dev(zz, xx):
        return (sec, zz * 2 + xx, tp)

    right = dev(lax.rem(z + 1, nz), x)
    left = dev(lax.rem(z + nz - 1, nz), x)
    partner = dev(z, 1 - x)

    def peer(o):
        return (lax.rem(sec + o // ntp, nsec), ctx, lax.rem(tp + o % ntp, ntp))

    n_peers = nsec * ntp

    count = [0]

    def sem_id():
        count[0] += 1
        assert count[0] <= n_sems
        return count[0] - 1

    sent = []

    def copy(src, dst, i, to):
        return pltpu.make_async_remote_copy(
            src_ref=src, dst_ref=dst, send_sem=ssem.at[i], recv_sem=rsem.at[i], device_id=to, device_id_type=MESH
        )

    def send(src, dst, i, to):
        c = copy(src, dst, i, to)
        c.start()
        sent.append(c)

    def arrive(dst, i, frm):
        copy(dst, dst, i, frm).wait_recv()

    own_cols = pl.ds(pl.multiple_of(head * HEAD_DIM, HEAD_DIM), HEAD_DIM)
    own_rows = pl.ds(pl.multiple_of(sec * mrows, mrows), mrows)
    local = [
        pltpu.make_async_copy(src, dst, lsem.at[i])
        for i, (src, dst) in enumerate(
            (
                (k_in, kv.at[z, 0]),
                (v_in, kv.at[z, 1]),
                (q_in, qs.at[SELF, x]),
                (cq_in, qs.at[CROSS, x]),
                (mk_in.at[:, own_cols], mb.at[z, 0, own_rows, :]),
                (mv_in.at[:, own_cols], mb.at[z, 1, own_rows, :]),
                (sgrad, grads.at[SELF]),
                (cgrad, grads.at[CROSS]),
                (sgain, gains.at[SELF]),
                (cgain, gains.at[CROSS]),
            )
        )
    ]
    for c in local:
        c.start()

    barrier = pltpu.get_barrier_semaphore()
    everyone = [right, left, partner] + [peer(o) for o in range(1, n_peers)]
    for to in everyone:
        pl.semaphore_signal(barrier, inc=1, device_id=to, device_id_type=MESH)
    pl.semaphore_wait(barrier, len(everyone))

    def zoff(d):
        return lax.rem(z + nz + d, nz)

    EARLY, LATE = ((0, 0), (1, 1)), ((0, 1), (1, 0))
    neighbour = (right, left)

    def ring_ids():
        return {(s, d, j): sem_id() for s in range(1, half + 1) for d in range(2) for j in range(2) if s < half or d == j}

    def towards(d, s):
        return zoff(-s) if d == 0 else zoff(s)

    kv_ids, mb_ids = ring_ids(), ring_ids()

    def ring_send(buf, ids, s, pairs):
        for d, j in pairs:
            if (s, d, j) in ids:
                ref = buf.at[towards(d, s - 1), j]
                send(ref, ref, ids[s, d, j], neighbour[d])

    def ring_arrive(buf, ids, s, pairs):
        for d, j in pairs:
            if (s, d, j) in ids:
                arrive(buf.at[towards(d, s), j], ids[s, d, j], neighbour[1 - d])

    def ring_pass(buf, ids, s, pairs):
        for pair in pairs:
            ring_arrive(buf, ids, s, (pair,))
            ring_send(buf, ids, s + 1, (pair,))

    mem_ids = []
    for o in range(1, nsec):
        to = (lax.rem(sec + o, nsec), ctx, tp)
        cols = pl.ds(pl.multiple_of((lax.rem(sec + o, nsec) * ntp + tp) * HEAD_DIM, HEAD_DIM), HEAD_DIM)
        for j, src in enumerate((mk_in, mv_in)):
            i = sem_id()
            send(src.at[:, cols], mb.at[z, j, own_rows, :], i, to)
            mem_ids.append((o, j, i))
    for pairs in (EARLY, LATE):
        for d, j in pairs:
            send((k_in, v_in)[j], kv.at[z, j], kv_ids[1, d, j], neighbour[d])
    q_ids = [sem_id(), sem_id()]
    for a, src in enumerate((q_in, cq_in)):
        send(src, qs.at[a, x], q_ids[a], partner)

    acc[...] = jnp.zeros_like(acc)
    for a in (SELF, CROSS):
        for h in range(2):
            ml[a, h, 0:1, :] = jnp.full((1, rows), NEG, F32)
            ml[a, h, 1:2, :] = jnp.zeros((1, rows), F32)

    def query_positions(h, begin, width):
        lane = lax.broadcasted_iota(jnp.int32, (1, 128), 1)
        first = (z * 2 + h) * nsub + begin // 128
        return jnp.concatenate([bs[first + i] * 128 + lane for i in range(width // 128)], axis=1)

    def masked(s, slot, h, begin):
        width = s.shape[1]
        qpos = query_positions(h, begin, width)
        first = (slot * 2 + x) * nsub
        row = lax.broadcasted_iota(jnp.int32, (128, width), 0)
        out = []
        for kb in range(nsub):
            gone = row > qpos - bs[first + kb] * 128
            out.append(jnp.where(gone, NEG, s[kb * 128 : (kb + 1) * 128, :]))
        return jnp.concatenate(out, axis=0)

    def forward(a, h, keys, values_t, slot):
        s = dot(keys, qs[a, h], 1, 1)
        if slot is not None:
            s = masked(s, slot, h, 0)
        old = ml[a, h, 0:1, :]
        new = jnp.maximum(old, jnp.max(s, axis=0, keepdims=True))
        p = jnp.exp2((s - new) * C2)
        shrink = jnp.exp2((old - new) * C2)
        ml[a, h, 0:1, :] = new
        ml[a, h, 1:2, :] = ml[a, h, 1:2, :] * shrink + jnp.sum(p, axis=0, keepdims=True)
        acc[a, h] = acc[a, h] * shrink + dot(values_t, p.astype(BF16), 1, 0)

    def self_forward(slot, h):
        forward(SELF, h, kv[slot, 0], kv[slot, 1].T, slot)

    def both_halves(slot):
        def one(h, c):
            self_forward(slot, h)
            return c

        lax.fori_loop(0, 2, one, 0)

    per = rows // srows
    n_groups = nz // per

    def cross_group(g, j):
        return jnp.concatenate([mb[zoff(g * per - 1 + i), j] for i in range(per)], axis=0)

    def cross_forward(g):
        def one(h, c):
            forward(CROSS, h, cross_group(g, 0), cross_group(g, 1).T, None)
            return c

        lax.fori_loop(0, 2, one, 0)

    for c in local[:3]:
        c.wait()
    self_forward(z, x)
    for c in local[3:]:
        c.wait()
    for o, j, i in mem_ids:
        frm = lax.rem(sec + nsec - o, nsec)
        dst = mb.at[z, j, pl.ds(pl.multiple_of(frm * mrows, mrows), mrows), :]
        arrive(dst, i, (frm, ctx, tp))
    ring_send(mb, mb_ids, 1, EARLY + LATE)
    arrive(qs.at[SELF, 1 - x], q_ids[SELF], partner)
    for s in range(1, half):
        ring_pass(kv, kv_ids, s, EARLY)
        if s == 1:
            self_forward(z, 1 - x)
        else:
            both_halves(zoff(1 - s))
        ring_pass(kv, kv_ids, s, LATE)
        if s > 1:
            both_halves(zoff(s - 1))
        ring_pass(mb, mb_ids, s, EARLY + LATE)
        if s == 1:
            dq[...] = jnp.zeros_like(dq)
            for a in (SELF, CROSS):
                lifted[a] = (gains[a] * grads[a].astype(F32)).T
    arrive(qs.at[CROSS, 1 - x], q_ids[CROSS], partner)
    cross_forward(0)
    both_halves(zoff(1 - half))
    both_halves(zoff(half - 1))
    ring_arrive(kv, kv_ids, half, EARLY)
    self_forward(zoff(half), 1 - x)

    o_ids = [(sem_id(), sem_id()) for _ in range(2)]
    n_ids = [[sem_id() for _ in range(1, n_peers)] for _ in range(2)]
    do_ids = [(sem_id(), sem_id()) for _ in range(2)]
    dq_ids = [sem_id(), sem_id()]

    def normed(a, h):
        total = ml[a, h, 1:2, :]
        return acc[a, h] * (1.0 / total), ml[a, h, 0:1, :] * C2 + jnp.log2(total)

    def send_partial(a):
        o, lse = normed(a, 1 - x)
        osend[a] = o.astype(BF16)
        pack_rows(ostat.at[a], [lse])
        send(osend.at[a], orecv.at[a], o_ids[a][0], partner)
        send(ostat.at[a], ostat_r.at[a], o_ids[a][1], partner)

    def combine(a):
        o0, l0 = normed(a, x)
        arrive(orecv.at[a], o_ids[a][0], partner)
        arrive(ostat_r.at[a], o_ids[a][1], partner)
        l1 = unpack_rows(ostat_r[a], 0, nsub)
        top = jnp.maximum(l0, l1)
        w0, w1 = jnp.exp2(l0 - top), jnp.exp2(l1 - top)
        total = w0 + w1
        inv = 1.0 / total
        o = o0 * (w0 * inv) + orecv[a].astype(F32) * (w1 * inv)
        ot[a] = o
        lse = top + jnp.log2(total)
        pack_rows(dstat.at[a, x], [lse])
        pack_rows(
            nsend.at[a],
            [jnp.sum(o * o, axis=0, keepdims=True), jnp.sum(lifted[a] * o, axis=0, keepdims=True)],
        )
        for k in range(1, n_peers):
            send(nsend.at[a], nrecv.at[a, k - 1], n_ids[a][k - 1], peer(k))

    def norm(a, out):
        total = nsend[a]
        for k in range(1, n_peers):
            frm = (lax.rem(sec + nsec - k // ntp, nsec), ctx, lax.rem(tp + ntp - k % ntp, ntp))
            arrive(nrecv.at[a, k - 1], n_ids[a][k - 1], frm)
            total = total + nrecv[a, k - 1]
        scale = lax.rsqrt(unpack_rows(total, 0, nsub) / full + EPS)
        slope = unpack_rows(total, nsub, nsub) / full
        o = ot[a]
        g = (scale * (lifted[a] - o * (scale * scale * slope))).astype(BF16)
        do[a, x] = g
        delta = jnp.sum(g.astype(F32) * o, axis=0, keepdims=True)
        pack_rows(dstat.at[a, x, nsub : 2 * nsub], [delta])
        send(do.at[a, x], do.at[a, x], do_ids[a][0], partner)
        send(dstat.at[a, x], dstat.at[a, x], do_ids[a][1], partner)
        out[...] = (gains[a] * (o * scale).T).astype(BF16)

    send_partial(SELF)
    self_forward(zoff(half), x)
    ring_arrive(mb, mb_ids, half, EARLY)
    for g in range(1, n_groups):
        cross_forward(g)
    send_partial(CROSS)
    combine(SELF)
    combine(CROSS)
    norm(SELF, self_out)

    def backward(a, h, keys, values, keys_t, slot, into):
        dk = dv = None
        for t in range(rows // TQ):
            cols = slice(t * TQ, (t + 1) * TQ)
            q = qs[a, h, cols, :]
            g = do[a, h, :, cols]
            stat = dstat[a, h]
            lse = unpack_rows(stat, t * (TQ // 128), TQ // 128)
            delta = unpack_rows(stat, nsub + t * (TQ // 128), TQ // 128)
            s = dot(keys, q, 1, 1)
            if slot is not None:
                s = masked(s, slot, h, t * TQ)
            p = jnp.exp2(s * C2 - lse)
            ds = (p * (dot(values, g, 1, 0) - delta)).astype(BF16)
            dv_t = dot(p.astype(BF16), g, 1, 1)
            dk_t = dot(ds, q, 1, 0)
            dv = dv_t if dv is None else dv + dv_t
            dk = dk_t if dk is None else dk + dk_t
            dq[a, h, :, cols] = dq[a, h, :, cols] + dot(keys_t, ds, 1, 0)
        kacc[into, 0] = kacc[into, 0] + dk * SCALE
        kacc[into, 1] = kacc[into, 1] + dv

    def self_backward(slot, h, into):
        backward(SELF, h, kv[slot, 0], kv[slot, 1], kv[slot, 0].T, slot, into)

    rs_ids, mrs_ids = ring_ids(), ring_ids()

    def reduce_step(dist, part, recv, snd, ids):
        for d, j in LATE + EARLY:
            if (dist, d, j) in ids:
                own = part(d, j)
                if (dist + 1, d, j) in ids:
                    arrive(recv.at[d, dist, j], ids[dist + 1, d, j], neighbour[1 - d])
                    own = own + recv[d, dist, j].astype(F32)
                snd[d, dist - 1, j] = own.astype(BF16)
                send(snd.at[d, dist - 1, j], recv.at[d, dist - 1, j], ids[dist, d, j], neighbour[d])

    def do_arrive(a):
        arrive(do.at[a, 1 - x], do_ids[a][0], partner)
        arrive(dstat.at[a, 1 - x], do_ids[a][1], partner)

    def cross_backward():
        def one(g, c):
            kacc[0] = jnp.zeros_like(kacc[0])
            keys_t = cross_group(g, 0).T

            def each(h, c2):
                backward(CROSS, h, cross_group(g, 0), cross_group(g, 1), keys_t, None, 0)
                return c2

            lax.fori_loop(0, 2, each, 0)
            for j in range(2):
                ms[pl.ds(g * per, per), j] = kacc[0, j].reshape(per, srows, HEAD_DIM)
            return c

        lax.fori_loop(0, n_groups, one, 0)

    def mem_own(dist, d, j):
        return ms[((dist if d == 0 else nz - dist) + 1) % nz, j]

    def mem_step(dist):
        reduce_step(dist, functools.partial(mem_own, dist), mrs_r, mrs_s, mrs_ids)

    def self_step(dist):
        reduce_step(dist, lambda d, j: kacc[0 if dist == half else 1 + d, j], rs_r, rs_s, rs_ids)

    def back_pair(dist, halves):
        def one(i, c):
            d, h = i // len(halves), i % len(halves)
            h = halves[0] if len(halves) == 1 else h
            self_backward(zoff((1 - 2 * d) * dist), h, 1 + d)
            return c

        lax.fori_loop(0, 2 * len(halves), one, 0)

    kacc[...] = jnp.zeros_like(kacc)
    self_backward(zoff(half), x, 0)
    norm(CROSS, cross_out)
    back_pair(half - 1, (x,))
    do_arrive(SELF)
    self_backward(zoff(half), 1 - x, 0)
    self_step(half)
    back_pair(half - 1, (1 - x,))
    self_step(half - 1)
    do_arrive(CROSS)
    cross_backward()
    mem_step(half)
    dqs[CROSS] = dq[CROSS, 1 - x].astype(BF16)
    send(dqs.at[CROSS], dqr.at[CROSS], dq_ids[CROSS], partner)
    for dist in range(half - 2, 0, -1):
        if dist == 1:
            kacc[0] = jnp.zeros_like(kacc[0])

            def back_own(h, c):
                self_backward(z, h, 0)
                return c

            lax.fori_loop(0, 2, back_own, 0)
            mem_step(2)
        kacc[1:3] = jnp.zeros_like(kacc[1:3])
        back_pair(dist, (0, 1))
        self_step(dist)
        if dist > 1:
            mem_step(dist + 1)
    dqs[SELF] = dq[SELF, 1 - x].astype(BF16)
    send(dqs.at[SELF], dqr.at[SELF], dq_ids[SELF], partner)
    mem_step(1)

    def reduced(own, recv, ids, j):
        for d in range(2):
            arrive(recv.at[d, 0, j], ids[1, d, j], neighbour[1 - d])
            own = own + recv[d, 0, j].astype(F32)
        return own.astype(BF16)

    def finish_query(a, out):
        arrive(dqr.at[a], dq_ids[a], partner)
        out[...] = ((dq[a, x] + dqr[a].astype(F32)) * SCALE).T.astype(BF16)

    finish_query(CROSS, cross_query_grad)
    for j in range(2):
        mfin[j] = reduced(ms[1, j], mrs_r, mrs_ids, j)
    ret_ids = [sem_id() for _ in range(1, n_peers)]
    for k in range(1, n_peers):
        to = peer(k)
        src_rows = pl.ds(pl.multiple_of(to[0] * mrows, mrows), mrows)
        send(mfin.at[:, src_rows, :], mout.at[:, :, own_cols], ret_ids[k - 1], to)
    mine = pltpu.make_async_copy(mfin.at[:, own_rows, :], mout.at[:, :, own_cols], lsem.at[0])
    mine.start()
    key_grad[...] = reduced(kacc[0, 0], rs_r, rs_ids, 0)
    value_grad[...] = reduced(kacc[0, 1], rs_r, rs_ids, 1)
    finish_query(SELF, query_grad)
    mine.wait()
    for k in range(1, n_peers):
        fs, ft = lax.rem(sec + nsec - k // ntp, nsec), lax.rem(tp + ntp - k % ntp, ntp)
        cols = pl.ds(pl.multiple_of((fs * ntp + ft) * HEAD_DIM, HEAD_DIM), HEAD_DIM)
        arrive(mout.at[:, :, cols], ret_ids[k - 1], (fs, ctx, ft))
    mkey_grad[...] = mout[0]
    mvalue_grad[...] = mout[1]
    for c in sent:
        c.wait_send()


def write_out(*refs):
    sems, stage = refs[-1], refs[16:24]
    ins = [pltpu.make_async_copy(refs[i], stage[i], sems.at[0, i]) for i in range(8)]
    outs = [pltpu.make_async_copy(stage[i], refs[8 + i], sems.at[1, i]) for i in range(8)]
    for c in ins:
        c.start()
    for c, d in zip(ins, outs):
        c.wait()
        d.start()
    for d in outs:
        d.wait()


def per_device(nz, nsec, ntp, *args):
    (sq, sk, sv, sgain, sgrad, cq, mk, mv, cgain, cgrad, bs) = args
    rows = sq.shape[0]
    mrows = mk.shape[0]
    half = nz // 2
    srows = nsec * mrows
    n_sems = 160
    hbm = pl.BlockSpec(memory_space=pltpu.HBM)
    vmem = pl.BlockSpec(memory_space=pltpu.VMEM)
    smem = pl.BlockSpec(memory_space=pltpu.SMEM)
    frame = jax.ShapeDtypeStruct((rows, HEAD_DIM), BF16)
    memory = jax.ShapeDtypeStruct(mk.shape, BF16)
    V = pltpu.VMEM
    results = pl.pallas_call(
        functools.partial(kernel, nz, nsec, ntp, n_sems),
        out_shape=(frame, frame, frame, frame, frame, frame, memory, memory),
        in_specs=[smem] + [hbm] * 10,
        out_specs=(vmem,) * 8,
        scratch_shapes=[
            V((nz, 2, rows, HEAD_DIM), BF16),
            V((2, 2, rows, HEAD_DIM), BF16),
            V((nz, 2, srows, HEAD_DIM), BF16),
            V((2, 2, HEAD_DIM, rows), F32),
            V((2, 2, 8, rows), F32),
            V((2, HEAD_DIM, rows), F32),
            V((2, HEAD_DIM, rows), F32),
            V((2, HEAD_DIM, rows), BF16),
            V((2, HEAD_DIM, rows), BF16),
            V((2, 8, 128), F32),
            V((2, 8, 128), F32),
            V((2, 8, 128), F32),
            V((2, nsec * ntp, 8, 128), F32),
            V((2, 2, HEAD_DIM, rows), BF16),
            V((2, 2, 8, 128), F32),
            V((2, 2, HEAD_DIM, rows), F32),
            V((2, HEAD_DIM, rows), BF16),
            V((2, HEAD_DIM, rows), BF16),
            V((3, 2, rows, HEAD_DIM), F32),
            V((2, half, 2, rows, HEAD_DIM), BF16),
            V((2, half, 2, rows, HEAD_DIM), BF16),
            V((nz, 2, srows, HEAD_DIM), F32),
            V((2, half, 2, srows, HEAD_DIM), BF16),
            V((2, half, 2, srows, HEAD_DIM), BF16),
            V((2, srows, HEAD_DIM), BF16),
            V((2, mrows, nsec * ntp * HEAD_DIM), BF16),
            V((2, rows, HEAD_DIM), BF16),
            V((2, 1, HEAD_DIM), F32),
            pltpu.SemaphoreType.DMA((n_sems,)),
            pltpu.SemaphoreType.DMA((n_sems,)),
            pltpu.SemaphoreType.DMA((10,)),
        ],
        compiler_params=pltpu.CompilerParams(
            collective_id=0, has_side_effects=True, vmem_limit_bytes=56 * 1024 * 1024
        ),
        cost_estimate=pl.CostEstimate(flops=9_000_000_000, bytes_accessed=4_000_000, transcendentals=10_000_000),
    )(bs, sq, sk, sv, sgain.reshape(1, -1), sgrad, cq, mk, mv, cgain.reshape(1, -1), cgrad)
    spec = pl.BlockSpec(memory_space=pl.ANY)
    return pl.pallas_call(
        write_out,
        out_shape=tuple(jax.ShapeDtypeStruct(r.shape, r.dtype) for r in results),
        in_specs=[spec] * 8,
        out_specs=(spec,) * 8,
        scratch_shapes=[V(r.shape, r.dtype) for r in results] + [pltpu.SemaphoreType.DMA((2, 8))],
        compiler_params=pltpu.CompilerParams(vmem_limit_bytes=56 * 1024 * 1024),
    )(*results)


def solution(mesh):
    nz, nsec, ntp = mesh.shape["ctx"] // 2, mesh.shape["sec"], mesh.shape["tp"]
    heads = ("sec", "tp")
    frame, gain, memory = P("ctx", heads), P(heads), P(("sec", "ctx"), None)
    return jax.shard_map(
        functools.partial(per_device, nz, nsec, ntp),
        mesh=mesh,
        in_specs=(frame, frame, frame, gain, frame, frame, memory, memory, gain, frame, P()),
        out_specs=(frame,) * 6 + (memory,) * 2,
        check_vma=False,
    )
```

```python
import functools
import math

import jax
import jax.numpy as jnp
from jax import lax
from jax.experimental import pallas as pl
from jax.experimental.pallas import tpu as pltpu
from jax.sharding import PartitionSpec as P

HEAD_DIM = 128
EPS = 1e-06
NEG = -1e30
SCALE = 1.0 / math.sqrt(HEAD_DIM)
C2 = SCALE * math.log2(math.e)
TQ = 256
MESH = pl.DeviceIdType.MESH
F32 = jnp.float32
BF16 = jnp.bfloat16
SELF, CROSS = 0, 1


def dot(a, b, ca, cb):
    return lax.dot_general(a, b, (((ca,), (cb,)), ((), ())), preferred_element_type=F32)


def pack_rows(ref, vectors):
    row = 0
    for v in vectors:
        for i in range(v.shape[1] // 128):
            ref[row : row + 1, :] = v[:, i * 128 : (i + 1) * 128]
            row += 1


def unpack_rows(tile, row, count):
    return jnp.concatenate([tile[row + i : row + i + 1, :] for i in range(count)], axis=1)


def kernel(
    nz, nsec, ntp, n_sems,
    bs, q_in, k_in, v_in, sgain, sgrad, cq_in, mk_in, mv_in, cgain, cgrad,
    self_out, cross_out, query_grad, key_grad, value_grad, cross_query_grad, mkey_grad, mvalue_grad,
    kv, qs, mb, acc, ml, ot, lifted, osend, orecv, ostat, ostat_r, nsend, nrecv, do, dstat,
    dq, dqs, dqr, kacc, rs_s, rs_r, ms, mrs_s, mrs_r, mfin, mout,
    grads, gains,
    ssem, rsem, lsem,
):
    rows = q_in.shape[0]
    mrows = mk_in.shape[0]
    srows = nsec * mrows
    half = nz // 2
    full = nsec * ntp * HEAD_DIM
    nsub = rows // 128

    sec, ctx, tp = lax.axis_index("sec"), lax.axis_index("ctx"), lax.axis_index("tp")
    z, x = ctx // 2, ctx % 2
    head = sec * ntp + tp

    def dev(zz, xx):
        return (sec, zz * 2 + xx, tp)

    right = dev(lax.rem(z + 1, nz), x)
    left = dev(lax.rem(z + nz - 1, nz), x)
    partner = dev(z, 1 - x)

    def peer(o):
        return (lax.rem(sec + o // ntp, nsec), ctx, lax.rem(tp + o % ntp, ntp))

    n_peers = nsec * ntp

    count = [0]

    def sem_id():
        count[0] += 1
        assert count[0] <= n_sems
        return count[0] - 1

    sent = []

    def copy(src, dst, i, to):
        return pltpu.make_async_remote_copy(
            src_ref=src, dst_ref=dst, send_sem=ssem.at[i], recv_sem=rsem.at[i], device_id=to, device_id_type=MESH
        )

    def send(src, dst, i, to):
        c = copy(src, dst, i, to)
        c.start()
        sent.append(c)

    def arrive(dst, i, frm):
        copy(dst, dst, i, frm).wait_recv()

    own_cols = pl.ds(pl.multiple_of(head * HEAD_DIM, HEAD_DIM), HEAD_DIM)
    own_rows = pl.ds(pl.multiple_of(sec * mrows, mrows), mrows)
    local = [
        pltpu.make_async_copy(src, dst, lsem.at[i])
        for i, (src, dst) in enumerate(
            (
                (k_in, kv.at[z, 0]),
                (v_in, kv.at[z, 1]),
                (q_in, qs.at[SELF, x]),
                (cq_in, qs.at[CROSS, x]),
                (mk_in.at[:, own_cols], mb.at[z, 0, own_rows, :]),
                (mv_in.at[:, own_cols], mb.at[z, 1, own_rows, :]),
                (sgrad, grads.at[SELF]),
                (cgrad, grads.at[CROSS]),
                (sgain, gains.at[SELF]),
                (cgain, gains.at[CROSS]),
            )
        )
    ]
    for c in local:
        c.start()

    barrier = pltpu.get_barrier_semaphore()
    everyone = [right, left, partner] + [peer(o) for o in range(1, n_peers)]
    for to in everyone:
        pl.semaphore_signal(barrier, inc=1, device_id=to, device_id_type=MESH)
    pl.semaphore_wait(barrier, len(everyone))

    def zoff(d):
        return lax.rem(z + nz + d, nz)

    EARLY, LATE = ((0, 0), (1, 1)), ((0, 1), (1, 0))
    neighbour = (right, left)

    def ring_ids():
        return {(s, d, j): sem_id() for s in range(1, half + 1) for d in range(2) for j in range(2) if s < half or d == j}

    def towards(d, s):
        return zoff(-s) if d == 0 else zoff(s)

    kv_ids, mb_ids = ring_ids(), ring_ids()

    def ring_send(buf, ids, s, pairs):
        for d, j in pairs:
            if (s, d, j) in ids:
                ref = buf.at[towards(d, s - 1), j]
                send(ref, ref, ids[s, d, j], neighbour[d])

    def ring_arrive(buf, ids, s, pairs):
        for d, j in pairs:
            if (s, d, j) in ids:
                arrive(buf.at[towards(d, s), j], ids[s, d, j], neighbour[1 - d])

    def ring_pass(buf, ids, s, pairs):
        for pair in pairs:
            ring_arrive(buf, ids, s, (pair,))
            ring_send(buf, ids, s + 1, (pair,))

    mem_ids = []
    for o in range(1, nsec):
        to = (lax.rem(sec + o, nsec), ctx, tp)
        cols = pl.ds(pl.multiple_of((lax.rem(sec + o, nsec) * ntp + tp) * HEAD_DIM, HEAD_DIM), HEAD_DIM)
        for j, src in enumerate((mk_in, mv_in)):
            i = sem_id()
            send(src.at[:, cols], mb.at[z, j, own_rows, :], i, to)
            mem_ids.append((o, j, i))
    for pairs in (EARLY, LATE):
        for d, j in pairs:
            send((k_in, v_in)[j], kv.at[z, j], kv_ids[1, d, j], neighbour[d])
    q_ids = [sem_id(), sem_id()]
    for a, src in enumerate((q_in, cq_in)):
        send(src, qs.at[a, x], q_ids[a], partner)

    acc[...] = jnp.zeros_like(acc)
    for a in (SELF, CROSS):
        for h in range(2):
            ml[a, h, 0:1, :] = jnp.full((1, rows), NEG, F32)
            ml[a, h, 1:2, :] = jnp.zeros((1, rows), F32)

    def query_positions(h, begin, width):
        lane = lax.broadcasted_iota(jnp.int32, (1, 128), 1)
        first = (z * 2 + h) * nsub + begin // 128
        return jnp.concatenate([bs[first + i] * 128 + lane for i in range(width // 128)], axis=1)

    def masked(s, slot, h, begin):
        width = s.shape[1]
        qpos = query_positions(h, begin, width)
        first = (slot * 2 + x) * nsub
        row = lax.broadcasted_iota(jnp.int32, (128, width), 0)
        out = []
        for kb in range(nsub):
            gone = row > qpos - bs[first + kb] * 128
            out.append(jnp.where(gone, NEG, s[kb * 128 : (kb + 1) * 128, :]))
        return jnp.concatenate(out, axis=0)

    def forward(a, h, keys, values_t, slot):
        s = dot(keys, qs[a, h], 1, 1)
        if slot is not None:
            s = masked(s, slot, h, 0)
        old = ml[a, h, 0:1, :]
        new = jnp.maximum(old, jnp.max(s, axis=0, keepdims=True))
        p = jnp.exp2((s - new) * C2)
        shrink = jnp.exp2((old - new) * C2)
        ml[a, h, 0:1, :] = new
        ml[a, h, 1:2, :] = ml[a, h, 1:2, :] * shrink + jnp.sum(p, axis=0, keepdims=True)
        acc[a, h] = acc[a, h] * shrink + dot(values_t, p.astype(BF16), 1, 0)

    def self_forward(slot, h):
        forward(SELF, h, kv[slot, 0], kv[slot, 1].T, slot)

    def both_halves(slot):
        def one(h, c):
            self_forward(slot, h)
            return c

        lax.fori_loop(0, 2, one, 0)

    per = rows // srows
    n_groups = nz // per

    def cross_group(g, j):
        return jnp.concatenate([mb[zoff(g * per - 1 + i), j] for i in range(per)], axis=0)

    def cross_forward(g):
        def one(h, c):
            forward(CROSS, h, cross_group(g, 0), cross_group(g, 1).T, None)
            return c

        lax.fori_loop(0, 2, one, 0)

    for c in local[:3]:
        c.wait()
    self_forward(z, x)
    for c in local[3:]:
        c.wait()
    for o, j, i in mem_ids:
        frm = lax.rem(sec + nsec - o, nsec)
        dst = mb.at[z, j, pl.ds(pl.multiple_of(frm * mrows, mrows), mrows), :]
        arrive(dst, i, (frm, ctx, tp))
    ring_send(mb, mb_ids, 1, EARLY + LATE)
    arrive(qs.at[SELF, 1 - x], q_ids[SELF], partner)
    for s in range(1, half):
        ring_pass(kv, kv_ids, s, EARLY)
        if s == 1:
            self_forward(z, 1 - x)
        else:
            both_halves(zoff(1 - s))
        ring_pass(kv, kv_ids, s, LATE)
        if s > 1:
            both_halves(zoff(s - 1))
        ring_pass(mb, mb_ids, s, EARLY + LATE)
        if s == 1:
            dq[...] = jnp.zeros_like(dq)
            for a in (SELF, CROSS):
                lifted[a] = (gains[a] * grads[a].astype(F32)).T
    arrive(qs.at[CROSS, 1 - x], q_ids[CROSS], partner)
    cross_forward(0)
    both_halves(zoff(1 - half))
    both_halves(zoff(half - 1))
    ring_arrive(kv, kv_ids, half, EARLY)
    self_forward(zoff(half), 1 - x)

    o_ids = [(sem_id(), sem_id()) for _ in range(2)]
    n_ids = [[sem_id() for _ in range(1, n_peers)] for _ in range(2)]
    do_ids = [(sem_id(), sem_id()) for _ in range(2)]
    dq_ids = [sem_id(), sem_id()]

    def normed(a, h):
        total = ml[a, h, 1:2, :]
        return acc[a, h] * (1.0 / total), ml[a, h, 0:1, :] * C2 + jnp.log2(total)

    def send_partial(a):
        o, lse = normed(a, 1 - x)
        osend[a] = o.astype(BF16)
        pack_rows(ostat.at[a], [lse])
        send(osend.at[a], orecv.at[a], o_ids[a][0], partner)
        send(ostat.at[a], ostat_r.at[a], o_ids[a][1], partner)

    def combine(a):
        o0, l0 = normed(a, x)
        arrive(orecv.at[a], o_ids[a][0], partner)
        arrive(ostat_r.at[a], o_ids[a][1], partner)
        l1 = unpack_rows(ostat_r[a], 0, nsub)
        top = jnp.maximum(l0, l1)
        w0, w1 = jnp.exp2(l0 - top), jnp.exp2(l1 - top)
        total = w0 + w1
        inv = 1.0 / total
        o = o0 * (w0 * inv) + orecv[a].astype(F32) * (w1 * inv)
        ot[a] = o
        lse = top + jnp.log2(total)
        pack_rows(dstat.at[a, x], [lse])
        pack_rows(
            nsend.at[a],
            [jnp.sum(o * o, axis=0, keepdims=True), jnp.sum(lifted[a] * o, axis=0, keepdims=True)],
        )
        for k in range(1, n_peers):
            send(nsend.at[a], nrecv.at[a, k - 1], n_ids[a][k - 1], peer(k))

    def norm(a, out):
        total = nsend[a]
        for k in range(1, n_peers):
            frm = (lax.rem(sec + nsec - k // ntp, nsec), ctx, lax.rem(tp + ntp - k % ntp, ntp))
            arrive(nrecv.at[a, k - 1], n_ids[a][k - 1], frm)
            total = total + nrecv[a, k - 1]
        scale = lax.rsqrt(unpack_rows(total, 0, nsub) / full + EPS)
        slope = unpack_rows(total, nsub, nsub) / full
        o = ot[a]
        g = (scale * (lifted[a] - o * (scale * scale * slope))).astype(BF16)
        do[a, x] = g
        delta = jnp.sum(g.astype(F32) * o, axis=0, keepdims=True)
        pack_rows(dstat.at[a, x, nsub : 2 * nsub], [delta])
        send(do.at[a, x], do.at[a, x], do_ids[a][0], partner)
        send(dstat.at[a, x], dstat.at[a, x], do_ids[a][1], partner)
        out[...] = (gains[a] * (o * scale).T).astype(BF16)

    send_partial(SELF)
    self_forward(zoff(half), x)
    ring_arrive(mb, mb_ids, half, EARLY)
    for g in range(1, n_groups):
        cross_forward(g)
    combine(SELF)
    send_partial(CROSS)
    norm(SELF, self_out)
    combine(CROSS)

    def backward(a, h, keys, values, keys_t, slot, keep):
        dk = dv = None
        for t in range(rows // TQ):
            cols = slice(t * TQ, (t + 1) * TQ)
            q = qs[a, h, cols, :]
            g = do[a, h, :, cols]
            stat = dstat[a, h]
            lse = unpack_rows(stat, t * (TQ // 128), TQ // 128)
            delta = unpack_rows(stat, nsub + t * (TQ // 128), TQ // 128)
            s = dot(keys, q, 1, 1)
            if slot is not None:
                s = masked(s, slot, h, t * TQ)
            p = jnp.exp2(s * C2 - lse)
            ds = (p * (dot(values, g, 1, 0) - delta)).astype(BF16)
            dv_t = dot(p.astype(BF16), g, 1, 1)
            dk_t = dot(ds, q, 1, 0)
            dv = dv_t if dv is None else dv + dv_t
            dk = dk_t if dk is None else dk + dk_t
            dq[a, h, :, cols] = dq[a, h, :, cols] + dot(keys_t, ds, 1, 0)
        keep(0, dk * SCALE)
        keep(1, dv)

    def self_backward(offset, h, first):
        slot = lax.rem(z + offset, nz)

        def keep(j, value):
            kacc[offset, j] = value if first else kacc[offset, j] + value

        backward(SELF, h, kv[slot, 0], kv[slot, 1], kv[slot, 0].T, slot, keep)

    def back_blocks(count, start, step, first):
        def one(i, c):
            self_backward(lax.rem(start + i * step, nz), x if first else 1 - x, first)
            return c

        lax.fori_loop(0, count, one, 0)

    rs_ids, mrs_ids = ring_ids(), ring_ids()

    def reduce_step(dist, part, recv, snd, ids, pairs):
        for d, j in pairs:
            if (dist, d, j) in ids:
                own = part(d, j)
                if (dist + 1, d, j) in ids:
                    arrive(recv.at[d, dist, j], ids[dist + 1, d, j], neighbour[1 - d])
                    own = own + recv[d, dist, j].astype(F32)
                snd[d, dist - 1, j] = own.astype(BF16)
                send(snd.at[d, dist - 1, j], recv.at[d, dist - 1, j], ids[dist, d, j], neighbour[d])

    def do_arrive(a):
        arrive(do.at[a, 1 - x], do_ids[a][0], partner)
        arrive(dstat.at[a, 1 - x], do_ids[a][1], partner)

    def cross_backward(first):
        def one(g, c):
            def keep(j, value):
                at = pl.ds(g * per, per)
                value = value.reshape(per, srows, HEAD_DIM)
                ms[at, j] = value if first else ms[at, j] + value

            keys = cross_group(g, 0)
            backward(CROSS, x if first else 1 - x, keys, cross_group(g, 1), keys.T, None, keep)
            return c

        lax.fori_loop(0, n_groups, one, 0)

    def mem_step(dist):
        def part(d, j):
            return ms[((dist if d == 0 else nz - dist) + 1) % nz, j]

        reduce_step(dist, part, mrs_r, mrs_s, mrs_ids, LATE + EARLY)

    def self_step(dist, pairs):
        reduce_step(dist, lambda d, j: kacc[dist if d == 0 else nz - dist, j], rs_r, rs_s, rs_ids, pairs)

    def send_query(a):
        dqs[a] = dq[a, 1 - x].astype(BF16)
        send(dqs.at[a], dqr.at[a], dq_ids[a], partner)

    back_blocks(3, half - 1, 1, True)
    for dist in range(half - 2, 1, -1):
        back_blocks(2, dist, nz - 2 * dist, True)
    do_arrive(SELF)
    back_blocks(1, half, 1, False)
    self_step(half, EARLY)
    norm(CROSS, cross_out)
    back_blocks(2, half - 1, 2, False)
    self_step(half - 1, LATE)
    back_blocks(3, nz - 1, 1, True)
    cross_backward(True)
    self_step(half - 1, EARLY)
    do_arrive(CROSS)
    cross_backward(False)
    mem_step(half)
    send_query(CROSS)
    for dist in range(half - 2, 1, -1):
        back_blocks(2, dist, nz - 2 * dist, False)
        mem_step(dist + 1)
        self_step(dist, LATE + EARLY)
    mem_step(2)
    back_blocks(3, nz - 1, 1, False)
    send_query(SELF)
    mem_step(1)
    self_step(1, LATE + EARLY)

    def reduced(own, recv, ids, j):
        for d in range(2):
            arrive(recv.at[d, 0, j], ids[1, d, j], neighbour[1 - d])
            own = own + recv[d, 0, j].astype(F32)
        return own.astype(BF16)

    def finish_query(a, out):
        arrive(dqr.at[a], dq_ids[a], partner)
        out[...] = ((dq[a, x] + dqr[a].astype(F32)) * SCALE).T.astype(BF16)

    finish_query(CROSS, cross_query_grad)
    for j in range(2):
        mfin[j] = reduced(ms[1, j], mrs_r, mrs_ids, j)
    ret_ids = [sem_id() for _ in range(1, n_peers)]
    for k in range(1, n_peers):
        to = peer(k)
        src_rows = pl.ds(pl.multiple_of(to[0] * mrows, mrows), mrows)
        send(mfin.at[:, src_rows, :], mout.at[:, :, own_cols], ret_ids[k - 1], to)
    mine = pltpu.make_async_copy(mfin.at[:, own_rows, :], mout.at[:, :, own_cols], lsem.at[0])
    mine.start()
    key_grad[...] = reduced(kacc[0, 0], rs_r, rs_ids, 0)
    value_grad[...] = reduced(kacc[0, 1], rs_r, rs_ids, 1)
    finish_query(SELF, query_grad)
    mine.wait()
    for k in range(1, n_peers):
        fs, ft = lax.rem(sec + nsec - k // ntp, nsec), lax.rem(tp + ntp - k % ntp, ntp)
        cols = pl.ds(pl.multiple_of((fs * ntp + ft) * HEAD_DIM, HEAD_DIM), HEAD_DIM)
        arrive(mout.at[:, :, cols], ret_ids[k - 1], (fs, ctx, ft))
    mkey_grad[...] = mout[0]
    mvalue_grad[...] = mout[1]
    for c in sent:
        c.wait_send()


def write_out(*refs):
    sems = refs[-1]
    copies = [pltpu.make_async_copy(refs[i], refs[8 + i], sems.at[i]) for i in range(8)]
    for c in copies:
        c.start()
    for c in copies:
        c.wait()


def per_device(nz, nsec, ntp, *args):
    (sq, sk, sv, sgain, sgrad, cq, mk, mv, cgain, cgrad, bs) = args
    rows = sq.shape[0]
    mrows = mk.shape[0]
    half = nz // 2
    srows = nsec * mrows
    n_sems = 160
    hbm = pl.BlockSpec(memory_space=pltpu.HBM)
    vmem = pl.BlockSpec(memory_space=pltpu.VMEM)
    smem = pl.BlockSpec(memory_space=pltpu.SMEM)
    V = pltpu.VMEM
    frame, memory = V((rows, HEAD_DIM), BF16), V(mk.shape, BF16)
    results = pl.pallas_call(
        functools.partial(kernel, nz, nsec, ntp, n_sems),
        out_shape=(frame, frame, frame, frame, frame, frame, memory, memory),
        in_specs=[smem] + [hbm] * 10,
        out_specs=(vmem,) * 8,
        scratch_shapes=[
            V((nz, 2, rows, HEAD_DIM), BF16),
            V((2, 2, rows, HEAD_DIM), BF16),
            V((nz, 2, srows, HEAD_DIM), BF16),
            V((2, 2, HEAD_DIM, rows), F32),
            V((2, 2, 8, rows), F32),
            V((2, HEAD_DIM, rows), F32),
            V((2, HEAD_DIM, rows), F32),
            V((2, HEAD_DIM, rows), BF16),
            V((2, HEAD_DIM, rows), BF16),
            V((2, 8, 128), F32),
            V((2, 8, 128), F32),
            V((2, 8, 128), F32),
            V((2, nsec * ntp, 8, 128), F32),
            V((2, 2, HEAD_DIM, rows), BF16),
            V((2, 2, 8, 128), F32),
            V((2, 2, HEAD_DIM, rows), F32),
            V((2, HEAD_DIM, rows), BF16),
            V((2, HEAD_DIM, rows), BF16),
            V((nz, 2, rows, HEAD_DIM), F32),
            V((2, half, 2, rows, HEAD_DIM), BF16),
            V((2, half, 2, rows, HEAD_DIM), BF16),
            V((nz, 2, srows, HEAD_DIM), F32),
            V((2, half, 2, srows, HEAD_DIM), BF16),
            V((2, half, 2, srows, HEAD_DIM), BF16),
            V((2, srows, HEAD_DIM), BF16),
            V((2, mrows, nsec * ntp * HEAD_DIM), BF16),
            V((2, rows, HEAD_DIM), BF16),
            V((2, 1, HEAD_DIM), F32),
            pltpu.SemaphoreType.DMA((n_sems,)),
            pltpu.SemaphoreType.DMA((n_sems,)),
            pltpu.SemaphoreType.DMA((10,)),
        ],
        compiler_params=pltpu.CompilerParams(
            collective_id=0, has_side_effects=True, vmem_limit_bytes=56 * 1024 * 1024
        ),
        cost_estimate=pl.CostEstimate(flops=9_000_000_000, bytes_accessed=4_000_000, transcendentals=10_000_000),
    )(bs, sq, sk, sv, sgain.reshape(1, -1), sgrad, cq, mk, mv, cgain.reshape(1, -1), cgrad)
    return pl.pallas_call(
        write_out,
        out_shape=tuple(jax.ShapeDtypeStruct(r.shape, r.dtype) for r in results),
        in_specs=[vmem] * 8,
        out_specs=(pl.BlockSpec(memory_space=pl.ANY),) * 8,
        scratch_shapes=[pltpu.SemaphoreType.DMA((8,))],
        compiler_params=pltpu.CompilerParams(vmem_limit_bytes=32 * 1024 * 1024),
    )(*results)


def solution(mesh):
    nz, nsec, ntp = mesh.shape["ctx"] // 2, mesh.shape["sec"], mesh.shape["tp"]
    heads = ("sec", "tp")
    frame, gain, memory = P("ctx", heads), P(heads), P(("sec", "ctx"), None)
    return jax.shard_map(
        functools.partial(per_device, nz, nsec, ntp),
        mesh=mesh,
        in_specs=(frame, frame, frame, gain, frame, frame, memory, memory, gain, frame, P()),
        out_specs=(frame,) * 6 + (memory,) * 2,
        check_vma=False,
    )
```

```python
import functools
import math

import jax
import jax.numpy as jnp
from jax import lax
from jax.experimental import pallas as pl
from jax.experimental.pallas import tpu as pltpu
from jax.sharding import PartitionSpec as P

HEAD_DIM = 128
EPS = 1e-06
NEG = -1e30
SCALE = 1.0 / math.sqrt(HEAD_DIM)
C2 = SCALE * math.log2(math.e)
TQ = 256
MESH = pl.DeviceIdType.MESH
F32 = jnp.float32
BF16 = jnp.bfloat16
SELF, CROSS = 0, 1


def dot(a, b, ca, cb):
    return lax.dot_general(a, b, (((ca,), (cb,)), ((), ())), preferred_element_type=F32)


def pack_rows(ref, vectors):
    row = 0
    for v in vectors:
        for i in range(v.shape[1] // 128):
            ref[row : row + 1, :] = v[:, i * 128 : (i + 1) * 128]
            row += 1


def unpack_rows(tile, row, count):
    return jnp.concatenate([tile[row + i : row + i + 1, :] for i in range(count)], axis=1)


def kernel(
    nz, nsec, ntp, n_sems,
    bs, q_in, k_in, v_in, sgain, sgrad, cq_in, mk_in, mv_in, cgain, cgrad,
    self_out, cross_out, query_grad, key_grad, value_grad, cross_query_grad, mkey_grad, mvalue_grad,
    kv, qs, mb, acc, ml, ot, lifted, osend, orecv, ostat, ostat_r, nsend, nrecv, do, dstat,
    dq, dqs, dqr, kacc, rs_s, rs_r, ms, mrs_s, mrs_r, mfin, mout,
    grads, gains,
    ssem, rsem, lsem,
):
    rows = q_in.shape[0]
    mrows = mk_in.shape[0]
    srows = nsec * mrows
    half = nz // 2
    full = nsec * ntp * HEAD_DIM
    nsub = rows // 128

    sec, ctx, tp = lax.axis_index("sec"), lax.axis_index("ctx"), lax.axis_index("tp")
    z, x = ctx // 2, ctx % 2
    head = sec * ntp + tp

    def dev(zz, xx):
        return (sec, zz * 2 + xx, tp)

    right = dev(lax.rem(z + 1, nz), x)
    left = dev(lax.rem(z + nz - 1, nz), x)
    partner = dev(z, 1 - x)

    def peer(o):
        return (lax.rem(sec + o // ntp, nsec), ctx, lax.rem(tp + o % ntp, ntp))

    n_peers = nsec * ntp

    count = [0]

    def sem_id():
        count[0] += 1
        assert count[0] <= n_sems
        return count[0] - 1

    sent = []

    def copy(src, dst, i, to):
        return pltpu.make_async_remote_copy(
            src_ref=src, dst_ref=dst, send_sem=ssem.at[i], recv_sem=rsem.at[i], device_id=to, device_id_type=MESH
        )

    def send(src, dst, i, to):
        c = copy(src, dst, i, to)
        c.start()
        sent.append(c)

    def arrive(dst, i, frm):
        copy(dst, dst, i, frm).wait_recv()

    own_cols = pl.ds(pl.multiple_of(head * HEAD_DIM, HEAD_DIM), HEAD_DIM)
    own_rows = pl.ds(pl.multiple_of(sec * mrows, mrows), mrows)
    local = [
        pltpu.make_async_copy(src, dst, lsem.at[i])
        for i, (src, dst) in enumerate(
            (
                (k_in, kv.at[z, 0]),
                (v_in, kv.at[z, 1]),
                (q_in, qs.at[SELF, x]),
                (cq_in, qs.at[CROSS, x]),
                (mk_in.at[:, own_cols], mb.at[z, 0, own_rows, :]),
                (mv_in.at[:, own_cols], mb.at[z, 1, own_rows, :]),
                (sgrad, grads.at[SELF]),
                (cgrad, grads.at[CROSS]),
                (sgain, gains.at[SELF]),
                (cgain, gains.at[CROSS]),
            )
        )
    ]
    for c in local:
        c.start()

    barrier = pltpu.get_barrier_semaphore()
    everyone = [right, left, partner] + [peer(o) for o in range(1, n_peers)]
    for to in everyone:
        pl.semaphore_signal(barrier, inc=1, device_id=to, device_id_type=MESH)
    pl.semaphore_wait(barrier, len(everyone))

    def zoff(d):
        return lax.rem(z + nz + d, nz)

    EARLY, LATE = ((0, 0), (1, 1)), ((0, 1), (1, 0))
    neighbour = (right, left)

    def ring_ids():
        return {(s, d, j): sem_id() for s in range(1, half + 1) for d in range(2) for j in range(2) if s < half or d == j}

    def towards(d, s):
        return zoff(-s) if d == 0 else zoff(s)

    kv_ids, mb_ids = ring_ids(), ring_ids()

    def ring_send(buf, ids, s, pairs):
        for d, j in pairs:
            if (s, d, j) in ids:
                ref = buf.at[towards(d, s - 1), j]
                send(ref, ref, ids[s, d, j], neighbour[d])

    def ring_arrive(buf, ids, s, pairs):
        for d, j in pairs:
            if (s, d, j) in ids:
                arrive(buf.at[towards(d, s), j], ids[s, d, j], neighbour[1 - d])

    def ring_pass(buf, ids, s, pairs):
        for pair in pairs:
            ring_arrive(buf, ids, s, (pair,))
            ring_send(buf, ids, s + 1, (pair,))

    mem_ids = []
    for o in range(1, nsec):
        to = (lax.rem(sec + o, nsec), ctx, tp)
        cols = pl.ds(pl.multiple_of((lax.rem(sec + o, nsec) * ntp + tp) * HEAD_DIM, HEAD_DIM), HEAD_DIM)
        for j, src in enumerate((mk_in, mv_in)):
            i = sem_id()
            send(src.at[:, cols], mb.at[z, j, own_rows, :], i, to)
            mem_ids.append((o, j, i))
    for pairs in (EARLY, LATE):
        for d, j in pairs:
            send((k_in, v_in)[j], kv.at[z, j], kv_ids[1, d, j], neighbour[d])
    q_ids = [sem_id(), sem_id()]
    for a, src in enumerate((q_in, cq_in)):
        send(src, qs.at[a, x], q_ids[a], partner)

    acc[...] = jnp.zeros_like(acc)
    for a in (SELF, CROSS):
        for h in range(2):
            ml[a, h, 0:1, :] = jnp.full((1, rows), NEG, F32)
            ml[a, h, 1:2, :] = jnp.zeros((1, rows), F32)

    def query_positions(h, begin, width):
        lane = lax.broadcasted_iota(jnp.int32, (1, 128), 1)
        first = (z * 2 + h) * nsub + begin // 128
        return jnp.concatenate([bs[first + i] * 128 + lane for i in range(width // 128)], axis=1)

    def masked(s, slot, h, begin):
        width = s.shape[1]
        qpos = query_positions(h, begin, width)
        first = (slot * 2 + x) * nsub
        row = lax.broadcasted_iota(jnp.int32, (128, width), 0)
        out = []
        for kb in range(nsub):
            gone = row > qpos - bs[first + kb] * 128
            out.append(jnp.where(gone, NEG, s[kb * 128 : (kb + 1) * 128, :]))
        return jnp.concatenate(out, axis=0)

    def forward(a, h, keys, values_t, slot):
        s = dot(keys, qs[a, h], 1, 1)
        if slot is not None:
            s = masked(s, slot, h, 0)
        old = ml[a, h, 0:1, :]
        new = jnp.maximum(old, jnp.max(s, axis=0, keepdims=True))
        p = jnp.exp2((s - new) * C2)
        shrink = jnp.exp2((old - new) * C2)
        ml[a, h, 0:1, :] = new
        ml[a, h, 1:2, :] = ml[a, h, 1:2, :] * shrink + jnp.sum(p, axis=0, keepdims=True)
        acc[a, h] = acc[a, h] * shrink + dot(values_t, p.astype(BF16), 1, 0)

    def self_forward(slot, h):
        forward(SELF, h, kv[slot, 0], kv[slot, 1].T, slot)

    def both_halves(slot):
        def one(h, c):
            self_forward(slot, h)
            return c

        lax.fori_loop(0, 2, one, 0)

    per = rows // srows
    n_groups = nz // per

    def cross_group(g, j):
        return jnp.concatenate([mb[zoff(g * per - 1 + i), j] for i in range(per)], axis=0)

    def cross_forward(g):
        def one(h, c):
            forward(CROSS, h, cross_group(g, 0), cross_group(g, 1).T, None)
            return c

        lax.fori_loop(0, 2, one, 0)

    for c in local[:3]:
        c.wait()
    self_forward(z, x)
    for c in local[3:]:
        c.wait()
    for o, j, i in mem_ids:
        frm = lax.rem(sec + nsec - o, nsec)
        dst = mb.at[z, j, pl.ds(pl.multiple_of(frm * mrows, mrows), mrows), :]
        arrive(dst, i, (frm, ctx, tp))
    ring_send(mb, mb_ids, 1, EARLY + LATE)
    arrive(qs.at[SELF, 1 - x], q_ids[SELF], partner)
    for s in range(1, half):
        ring_pass(kv, kv_ids, s, EARLY)
        if s == 1:
            self_forward(z, 1 - x)
        else:
            both_halves(zoff(1 - s))
        ring_pass(kv, kv_ids, s, LATE)
        if s > 1:
            both_halves(zoff(s - 1))
        if s < half - 1:
            ring_pass(mb, mb_ids, s, EARLY + LATE)
        if s == 1:
            dq[...] = jnp.zeros_like(dq)
            for a in (SELF, CROSS):
                lifted[a] = (gains[a] * grads[a].astype(F32)).T
    arrive(qs.at[CROSS, 1 - x], q_ids[CROSS], partner)
    cross_forward(0)
    both_halves(zoff(1 - half))
    both_halves(zoff(half - 1))
    ring_arrive(kv, kv_ids, half, EARLY)
    ring_pass(mb, mb_ids, half - 1, EARLY + LATE)
    self_forward(zoff(half), 1 - x)

    o_ids = [(sem_id(), sem_id()) for _ in range(2)]
    n_ids = [[sem_id() for _ in range(1, n_peers)] for _ in range(2)]
    do_ids = [(sem_id(), sem_id()) for _ in range(2)]
    dq_ids = [sem_id(), sem_id()]

    def normed(a, h):
        total = ml[a, h, 1:2, :]
        return acc[a, h] * (1.0 / total), ml[a, h, 0:1, :] * C2 + jnp.log2(total)

    def send_partial(a):
        o, lse = normed(a, 1 - x)
        osend[a] = o.astype(BF16)
        pack_rows(ostat.at[a], [lse])
        send(osend.at[a], orecv.at[a], o_ids[a][0], partner)
        send(ostat.at[a], ostat_r.at[a], o_ids[a][1], partner)

    def combine(a):
        o0, l0 = normed(a, x)
        arrive(orecv.at[a], o_ids[a][0], partner)
        arrive(ostat_r.at[a], o_ids[a][1], partner)
        l1 = unpack_rows(ostat_r[a], 0, nsub)
        top = jnp.maximum(l0, l1)
        w0, w1 = jnp.exp2(l0 - top), jnp.exp2(l1 - top)
        total = w0 + w1
        inv = 1.0 / total
        o = o0 * (w0 * inv) + orecv[a].astype(F32) * (w1 * inv)
        ot[a] = o
        lse = top + jnp.log2(total)
        pack_rows(dstat.at[a, x], [lse])
        pack_rows(
            nsend.at[a],
            [jnp.sum(o * o, axis=0, keepdims=True), jnp.sum(lifted[a] * o, axis=0, keepdims=True)],
        )
        for k in range(1, n_peers):
            send(nsend.at[a], nrecv.at[a, k - 1], n_ids[a][k - 1], peer(k))

    def norm(a, out):
        total = nsend[a]
        for k in range(1, n_peers):
            frm = (lax.rem(sec + nsec - k // ntp, nsec), ctx, lax.rem(tp + ntp - k % ntp, ntp))
            arrive(nrecv.at[a, k - 1], n_ids[a][k - 1], frm)
            total = total + nrecv[a, k - 1]
        scale = lax.rsqrt(unpack_rows(total, 0, nsub) / full + EPS)
        slope = unpack_rows(total, nsub, nsub) / full
        o = ot[a]
        g = (scale * (lifted[a] - o * (scale * scale * slope))).astype(BF16)
        do[a, x] = g
        delta = jnp.sum(g.astype(F32) * o, axis=0, keepdims=True)
        pack_rows(dstat.at[a, x, nsub : 2 * nsub], [delta])
        send(do.at[a, x], do.at[a, x], do_ids[a][0], partner)
        send(dstat.at[a, x], dstat.at[a, x], do_ids[a][1], partner)
        out[...] = (gains[a] * (o * scale).T).astype(BF16)

    send_partial(SELF)
    self_forward(zoff(half), x)
    ring_arrive(mb, mb_ids, half, EARLY)
    for g in range(1, n_groups):
        cross_forward(g)
    combine(SELF)
    send_partial(CROSS)
    norm(SELF, self_out)
    combine(CROSS)

    def backward(a, h, keys, values, keys_t, slot, keep):
        dk = dv = None
        for t in range(rows // TQ):
            cols = slice(t * TQ, (t + 1) * TQ)
            q = qs[a, h, cols, :]
            g = do[a, h, :, cols]
            stat = dstat[a, h]
            lse = unpack_rows(stat, t * (TQ // 128), TQ // 128)
            delta = unpack_rows(stat, nsub + t * (TQ // 128), TQ // 128)
            s = dot(keys, q, 1, 1)
            if slot is not None:
                s = masked(s, slot, h, t * TQ)
            p = jnp.exp2(s * C2 - lse)
            ds = (p * (dot(values, g, 1, 0) - delta)).astype(BF16)
            dv_t = dot(p.astype(BF16), g, 1, 1)
            dk_t = dot(ds, q, 1, 0)
            dv = dv_t if dv is None else dv + dv_t
            dk = dk_t if dk is None else dk + dk_t
            dq[a, h, :, cols] = dq[a, h, :, cols] + dot(keys_t, ds, 1, 0)
        keep(0, dk * SCALE)
        keep(1, dv)

    def self_backward(offset, h, first):
        slot = lax.rem(z + offset, nz)

        def keep(j, value):
            kacc[offset, j] = value if first else kacc[offset, j] + value

        backward(SELF, h, kv[slot, 0], kv[slot, 1], kv[slot, 0].T, slot, keep)

    def back_blocks(count, start, step, first):
        def one(i, c):
            self_backward(lax.rem(start + i * step, nz), x if first else 1 - x, first)
            return c

        lax.fori_loop(0, count, one, 0)

    rs_ids, mrs_ids = ring_ids(), ring_ids()

    def reduce_step(dist, part, recv, snd, ids, pairs):
        for d, j in pairs:
            if (dist, d, j) in ids:
                own = part(d, j)
                if (dist + 1, d, j) in ids:
                    arrive(recv.at[d, dist, j], ids[dist + 1, d, j], neighbour[1 - d])
                    own = own + recv[d, dist, j].astype(F32)
                snd[d, dist - 1, j] = own.astype(BF16)
                send(snd.at[d, dist - 1, j], recv.at[d, dist - 1, j], ids[dist, d, j], neighbour[d])

    def do_arrive(a):
        arrive(do.at[a, 1 - x], do_ids[a][0], partner)
        arrive(dstat.at[a, 1 - x], do_ids[a][1], partner)

    def cross_backward(first):
        def one(g, c):
            def keep(j, value):
                at = pl.ds(g * per, per)
                value = value.reshape(per, srows, HEAD_DIM)
                ms[at, j] = value if first else ms[at, j] + value

            keys = cross_group(g, 0)
            backward(CROSS, x if first else 1 - x, keys, cross_group(g, 1), keys.T, None, keep)
            return c

        lax.fori_loop(0, n_groups, one, 0)

    def mem_step(dist):
        def part(d, j):
            return ms[((dist if d == 0 else nz - dist) + 1) % nz, j]

        reduce_step(dist, part, mrs_r, mrs_s, mrs_ids, LATE + EARLY)

    def self_step(dist, pairs):
        reduce_step(dist, lambda d, j: kacc[dist if d == 0 else nz - dist, j], rs_r, rs_s, rs_ids, pairs)

    def send_query(a):
        dqs[a] = dq[a, 1 - x].astype(BF16)
        send(dqs.at[a], dqr.at[a], dq_ids[a], partner)

    back_blocks(3, half - 1, 1, True)
    for dist in range(half - 2, 1, -1):
        back_blocks(2, dist, nz - 2 * dist, True)
    norm(CROSS, cross_out)
    do_arrive(SELF)
    back_blocks(1, half, 1, False)
    self_step(half, EARLY)
    back_blocks(2, half - 1, 2, False)
    self_step(half - 1, LATE)
    cross_backward(True)
    do_arrive(CROSS)
    cross_backward(False)
    mem_step(half)
    self_step(half - 1, EARLY)
    send_query(CROSS)
    for dist in range(half - 2, 1, -1):
        back_blocks(2, dist, nz - 2 * dist, False)
        mem_step(dist + 1)
        self_step(dist, LATE + EARLY)
    mem_step(2)
    back_blocks(3, nz - 1, 1, True)
    back_blocks(3, nz - 1, 1, False)
    send_query(SELF)
    mem_step(1)
    self_step(1, LATE + EARLY)

    def reduced(own, recv, ids, j):
        for d in range(2):
            arrive(recv.at[d, 0, j], ids[1, d, j], neighbour[1 - d])
            own = own + recv[d, 0, j].astype(F32)
        return own.astype(BF16)

    def finish_query(a, out):
        arrive(dqr.at[a], dq_ids[a], partner)
        out[...] = ((dq[a, x] + dqr[a].astype(F32)) * SCALE).T.astype(BF16)

    finish_query(CROSS, cross_query_grad)
    for j in range(2):
        mfin[j] = reduced(ms[1, j], mrs_r, mrs_ids, j)
    ret_ids = [sem_id() for _ in range(1, n_peers)]
    for k in range(1, n_peers):
        to = peer(k)
        src_rows = pl.ds(pl.multiple_of(to[0] * mrows, mrows), mrows)
        send(mfin.at[:, src_rows, :], mout.at[:, :, own_cols], ret_ids[k - 1], to)
    mine = pltpu.make_async_copy(mfin.at[:, own_rows, :], mout.at[:, :, own_cols], lsem.at[0])
    mine.start()
    finish_query(SELF, query_grad)
    mine.wait()
    key_grad[...] = reduced(kacc[0, 0], rs_r, rs_ids, 0)
    value_grad[...] = reduced(kacc[0, 1], rs_r, rs_ids, 1)
    for k in range(1, n_peers):
        fs, ft = lax.rem(sec + nsec - k // ntp, nsec), lax.rem(tp + ntp - k % ntp, ntp)
        cols = pl.ds(pl.multiple_of((fs * ntp + ft) * HEAD_DIM, HEAD_DIM), HEAD_DIM)
        arrive(mout.at[:, :, cols], ret_ids[k - 1], (fs, ctx, ft))
    mkey_grad[...] = mout[0]
    mvalue_grad[...] = mout[1]
    for c in sent:
        c.wait_send()


def write_out(*refs):
    sems = refs[-1]
    copies = [pltpu.make_async_copy(refs[i], refs[8 + i], sems.at[i]) for i in range(8)]
    for c in copies:
        c.start()
    for c in copies:
        c.wait()


def per_device(nz, nsec, ntp, *args):
    (sq, sk, sv, sgain, sgrad, cq, mk, mv, cgain, cgrad, bs) = args
    rows = sq.shape[0]
    mrows = mk.shape[0]
    half = nz // 2
    srows = nsec * mrows
    n_sems = 160
    hbm = pl.BlockSpec(memory_space=pltpu.HBM)
    vmem = pl.BlockSpec(memory_space=pltpu.VMEM)
    smem = pl.BlockSpec(memory_space=pltpu.SMEM)
    V = pltpu.VMEM
    frame, memory = V((rows, HEAD_DIM), BF16), V(mk.shape, BF16)
    results = pl.pallas_call(
        functools.partial(kernel, nz, nsec, ntp, n_sems),
        out_shape=(frame, frame, frame, frame, frame, frame, memory, memory),
        in_specs=[smem] + [hbm] * 10,
        out_specs=(vmem,) * 8,
        scratch_shapes=[
            V((nz, 2, rows, HEAD_DIM), BF16),
            V((2, 2, rows, HEAD_DIM), BF16),
            V((nz, 2, srows, HEAD_DIM), BF16),
            V((2, 2, HEAD_DIM, rows), F32),
            V((2, 2, 8, rows), F32),
            V((2, HEAD_DIM, rows), F32),
            V((2, HEAD_DIM, rows), F32),
            V((2, HEAD_DIM, rows), BF16),
            V((2, HEAD_DIM, rows), BF16),
            V((2, 8, 128), F32),
            V((2, 8, 128), F32),
            V((2, 8, 128), F32),
            V((2, nsec * ntp, 8, 128), F32),
            V((2, 2, HEAD_DIM, rows), BF16),
            V((2, 2, 8, 128), F32),
            V((2, 2, HEAD_DIM, rows), F32),
            V((2, HEAD_DIM, rows), BF16),
            V((2, HEAD_DIM, rows), BF16),
            V((nz, 2, rows, HEAD_DIM), F32),
            V((2, half, 2, rows, HEAD_DIM), BF16),
            V((2, half, 2, rows, HEAD_DIM), BF16),
            V((nz, 2, srows, HEAD_DIM), F32),
            V((2, half, 2, srows, HEAD_DIM), BF16),
            V((2, half, 2, srows, HEAD_DIM), BF16),
            V((2, srows, HEAD_DIM), BF16),
            V((2, mrows, nsec * ntp * HEAD_DIM), BF16),
            V((2, rows, HEAD_DIM), BF16),
            V((2, 1, HEAD_DIM), F32),
            pltpu.SemaphoreType.DMA((n_sems,)),
            pltpu.SemaphoreType.DMA((n_sems,)),
            pltpu.SemaphoreType.DMA((10,)),
        ],
        compiler_params=pltpu.CompilerParams(
            collective_id=0, has_side_effects=True, vmem_limit_bytes=56 * 1024 * 1024
        ),
        cost_estimate=pl.CostEstimate(flops=9_000_000_000, bytes_accessed=4_000_000, transcendentals=10_000_000),
    )(bs, sq, sk, sv, sgain.reshape(1, -1), sgrad, cq, mk, mv, cgain.reshape(1, -1), cgrad)
    return pl.pallas_call(
        write_out,
        out_shape=tuple(jax.ShapeDtypeStruct(r.shape, r.dtype) for r in results),
        in_specs=[vmem] * 8,
        out_specs=(pl.BlockSpec(memory_space=pl.ANY),) * 8,
        scratch_shapes=[pltpu.SemaphoreType.DMA((8,))],
        compiler_params=pltpu.CompilerParams(vmem_limit_bytes=32 * 1024 * 1024),
    )(*results)


def solution(mesh):
    nz, nsec, ntp = mesh.shape["ctx"] // 2, mesh.shape["sec"], mesh.shape["tp"]
    heads = ("sec", "tp")
    frame, gain, memory = P("ctx", heads), P(heads), P(("sec", "ctx"), None)
    return jax.shard_map(
        functools.partial(per_device, nz, nsec, ntp),
        mesh=mesh,
        in_specs=(frame, frame, frame, gain, frame, frame, memory, memory, gain, frame, P()),
        out_specs=(frame,) * 6 + (memory,) * 2,
        check_vma=False,
    )
```

```python
import functools
import math

import jax
import jax.numpy as jnp
from jax import lax
from jax.experimental import pallas as pl
from jax.experimental.pallas import tpu as pltpu
from jax.sharding import PartitionSpec as P

HEAD_DIM = 128
EPS = 1e-06
NEG = -1e30
SCALE = 1.0 / math.sqrt(HEAD_DIM)
C2 = SCALE * math.log2(math.e)
TQ = 512
MESH = pl.DeviceIdType.MESH
F32 = jnp.float32
BF16 = jnp.bfloat16
SELF, CROSS = 0, 1


def dot(a, b, ca, cb):
    return lax.dot_general(a, b, (((ca,), (cb,)), ((), ())), preferred_element_type=F32)


def pack_rows(ref, vectors):
    row = 0
    for v in vectors:
        for i in range(v.shape[1] // 128):
            ref[row : row + 1, :] = v[:, i * 128 : (i + 1) * 128]
            row += 1


def unpack_rows(tile, row, count):
    return jnp.concatenate([tile[row + i : row + i + 1, :] for i in range(count)], axis=1)


def kernel(
    nz, nsec, ntp, n_sems,
    bs, q_in, k_in, v_in, sgain, sgrad, cq_in, mk_in, mv_in, cgain, cgrad,
    self_out, cross_out, query_grad, key_grad, value_grad, cross_query_grad, mkey_grad, mvalue_grad,
    kv, qs, mb, acc, ml, ot, lifted, osend, orecv, ostat, ostat_r, nsend, nrecv, do, dstat,
    dq, dqs, dqr, kacc, rs_s, rs_r, ms, mrs_s, mrs_r, mfin, mout,
    grads, gains,
    ssem, rsem, lsem,
):
    rows = q_in.shape[0]
    mrows = mk_in.shape[0]
    srows = nsec * mrows
    half = nz // 2
    full = nsec * ntp * HEAD_DIM
    nsub = rows // 128

    sec, ctx, tp = lax.axis_index("sec"), lax.axis_index("ctx"), lax.axis_index("tp")
    z, x = ctx // 2, ctx % 2
    head = sec * ntp + tp

    def dev(zz, xx):
        return (sec, zz * 2 + xx, tp)

    right = dev(lax.rem(z + 1, nz), x)
    left = dev(lax.rem(z + nz - 1, nz), x)
    partner = dev(z, 1 - x)

    def peer(o):
        return (lax.rem(sec + o // ntp, nsec), ctx, lax.rem(tp + o % ntp, ntp))

    n_peers = nsec * ntp

    count = [0]

    def sem_id():
        count[0] += 1
        assert count[0] <= n_sems
        return count[0] - 1

    sent = []

    def copy(src, dst, i, to):
        return pltpu.make_async_remote_copy(
            src_ref=src, dst_ref=dst, send_sem=ssem.at[i], recv_sem=rsem.at[i], device_id=to, device_id_type=MESH
        )

    def send(src, dst, i, to):
        c = copy(src, dst, i, to)
        c.start()
        sent.append(c)

    def arrive(dst, i, frm):
        copy(dst, dst, i, frm).wait_recv()

    own_cols = pl.ds(pl.multiple_of(head * HEAD_DIM, HEAD_DIM), HEAD_DIM)
    own_rows = pl.ds(pl.multiple_of(sec * mrows, mrows), mrows)
    local = [
        pltpu.make_async_copy(src, dst, lsem.at[i])
        for i, (src, dst) in enumerate(
            (
                (k_in, kv.at[z, 0]),
                (v_in, kv.at[z, 1]),
                (q_in, qs.at[SELF, x]),
                (cq_in, qs.at[CROSS, x]),
                (mk_in.at[:, own_cols], mb.at[z, 0, own_rows, :]),
                (mv_in.at[:, own_cols], mb.at[z, 1, own_rows, :]),
                (sgrad, grads.at[SELF]),
                (cgrad, grads.at[CROSS]),
                (sgain, gains.at[SELF]),
                (cgain, gains.at[CROSS]),
            )
        )
    ]
    for c in local:
        c.start()

    barrier = pltpu.get_barrier_semaphore()
    everyone = [right, left, partner] + [peer(o) for o in range(1, n_peers)]
    for to in everyone:
        pl.semaphore_signal(barrier, inc=1, device_id=to, device_id_type=MESH)
    pl.semaphore_wait(barrier, len(everyone))

    def zoff(d):
        return lax.rem(z + nz + d, nz)

    EARLY, LATE = ((0, 0), (1, 1)), ((0, 1), (1, 0))
    neighbour = (right, left)

    def ring_ids():
        return {(s, d, j): sem_id() for s in range(1, half + 1) for d in range(2) for j in range(2) if s < half or d == j}

    def towards(d, s):
        return zoff(-s) if d == 0 else zoff(s)

    kv_ids, mb_ids = ring_ids(), ring_ids()

    def ring_send(buf, ids, s, pairs):
        for d, j in pairs:
            if (s, d, j) in ids:
                ref = buf.at[towards(d, s - 1), j]
                send(ref, ref, ids[s, d, j], neighbour[d])

    def ring_arrive(buf, ids, s, pairs):
        for d, j in pairs:
            if (s, d, j) in ids:
                arrive(buf.at[towards(d, s), j], ids[s, d, j], neighbour[1 - d])

    def ring_pass(buf, ids, s, pairs):
        for pair in pairs:
            ring_arrive(buf, ids, s, (pair,))
            ring_send(buf, ids, s + 1, (pair,))

    mem_ids = []
    for o in range(1, nsec):
        to = (lax.rem(sec + o, nsec), ctx, tp)
        cols = pl.ds(pl.multiple_of((lax.rem(sec + o, nsec) * ntp + tp) * HEAD_DIM, HEAD_DIM), HEAD_DIM)
        for j, src in enumerate((mk_in, mv_in)):
            i = sem_id()
            send(src.at[:, cols], mb.at[z, j, own_rows, :], i, to)
            mem_ids.append((o, j, i))
    def first_send(pairs):
        for d, j in pairs:
            send((k_in, v_in)[j], kv.at[z, j], kv_ids[1, d, j], neighbour[d])

    first_send(EARLY)
    q_ids = [sem_id(), sem_id()]
    for a, src in enumerate((q_in, cq_in)):
        send(src, qs.at[a, x], q_ids[a], partner)

    acc[...] = jnp.zeros_like(acc)
    for a in (SELF, CROSS):
        for h in range(2):
            ml[a, h, 0:1, :] = jnp.full((1, rows), NEG, F32)
            ml[a, h, 1:2, :] = jnp.zeros((1, rows), F32)

    def query_positions(h, begin, width):
        lane = lax.broadcasted_iota(jnp.int32, (1, 128), 1)
        first = (z * 2 + h) * nsub + begin // 128
        return jnp.concatenate([bs[first + i] * 128 + lane for i in range(width // 128)], axis=1)

    def masked(s, slot, h, begin):
        width = s.shape[1]
        qpos = query_positions(h, begin, width)
        first = (slot * 2 + x) * nsub
        row = lax.broadcasted_iota(jnp.int32, (128, width), 0)
        out = []
        for kb in range(nsub):
            gone = row > qpos - bs[first + kb] * 128
            out.append(jnp.where(gone, NEG, s[kb * 128 : (kb + 1) * 128, :]))
        return jnp.concatenate(out, axis=0)

    def forward(a, h, keys, values_t, slot):
        s = dot(keys, qs[a, h], 1, 1)
        if slot is not None:
            s = masked(s, slot, h, 0)
        old = ml[a, h, 0:1, :]
        new = jnp.maximum(old, jnp.max(s, axis=0, keepdims=True))
        p = jnp.exp2((s - new) * C2)
        shrink = jnp.exp2((old - new) * C2)
        ml[a, h, 0:1, :] = new
        ml[a, h, 1:2, :] = ml[a, h, 1:2, :] * shrink + jnp.sum(p, axis=0, keepdims=True)
        acc[a, h] = acc[a, h] * shrink + dot(values_t, p.astype(BF16), 1, 0)

    def self_forward(slot, h):
        forward(SELF, h, kv[slot, 0], kv[slot, 1].T, slot)

    def both_halves(slot):
        def one(h, c):
            self_forward(slot, h)
            return c

        lax.fori_loop(0, 2, one, 0)

    per = rows // srows
    n_groups = nz // per

    def cross_group(g, j):
        return jnp.concatenate([mb[zoff(g * per - 1 + i), j] for i in range(per)], axis=0)

    def cross_forward(g):
        def one(h, c):
            forward(CROSS, h, cross_group(g, 0), cross_group(g, 1).T, None)
            return c

        lax.fori_loop(0, 2, one, 0)

    for c in local[:3]:
        c.wait()
    self_forward(z, x)
    first_send(LATE)
    for c in local[3:]:
        c.wait()
    for o, j, i in mem_ids:
        frm = lax.rem(sec + nsec - o, nsec)
        dst = mb.at[z, j, pl.ds(pl.multiple_of(frm * mrows, mrows), mrows), :]
        arrive(dst, i, (frm, ctx, tp))
    ring_send(mb, mb_ids, 1, EARLY + LATE)
    arrive(qs.at[SELF, 1 - x], q_ids[SELF], partner)
    for s in range(1, half):
        ring_pass(kv, kv_ids, s, EARLY)
        if s == 1:
            self_forward(z, 1 - x)
        else:
            both_halves(zoff(1 - s))
        ring_pass(kv, kv_ids, s, LATE)
        if s > 1:
            both_halves(zoff(s - 1))
        if s < half - 1:
            ring_pass(mb, mb_ids, s, EARLY + LATE)
        if s == 1:
            dq[...] = jnp.zeros_like(dq)
            for a in (SELF, CROSS):
                lifted[a] = (gains[a] * grads[a].astype(F32)).T
    arrive(qs.at[CROSS, 1 - x], q_ids[CROSS], partner)
    cross_forward(0)
    both_halves(zoff(1 - half))
    both_halves(zoff(half - 1))
    ring_arrive(kv, kv_ids, half, EARLY)
    ring_pass(mb, mb_ids, half - 1, EARLY + LATE)
    self_forward(zoff(half), 1 - x)

    o_ids = [(sem_id(), sem_id()) for _ in range(2)]
    n_ids = [[sem_id() for _ in range(1, n_peers)] for _ in range(2)]
    do_ids = [(sem_id(), sem_id()) for _ in range(2)]
    dq_ids = [sem_id(), sem_id()]

    def normed(a, h):
        total = ml[a, h, 1:2, :]
        return acc[a, h] * (1.0 / total), ml[a, h, 0:1, :] * C2 + jnp.log2(total)

    def send_partial(a):
        o, lse = normed(a, 1 - x)
        osend[a] = o.astype(BF16)
        pack_rows(ostat.at[a], [lse])
        send(osend.at[a], orecv.at[a], o_ids[a][0], partner)
        send(ostat.at[a], ostat_r.at[a], o_ids[a][1], partner)

    def combine(a):
        o0, l0 = normed(a, x)
        arrive(orecv.at[a], o_ids[a][0], partner)
        arrive(ostat_r.at[a], o_ids[a][1], partner)
        l1 = unpack_rows(ostat_r[a], 0, nsub)
        top = jnp.maximum(l0, l1)
        w0, w1 = jnp.exp2(l0 - top), jnp.exp2(l1 - top)
        total = w0 + w1
        inv = 1.0 / total
        o = o0 * (w0 * inv) + orecv[a].astype(F32) * (w1 * inv)
        ot[a] = o
        lse = top + jnp.log2(total)
        pack_rows(dstat.at[a, x], [lse])
        pack_rows(
            nsend.at[a],
            [jnp.sum(o * o, axis=0, keepdims=True), jnp.sum(lifted[a] * o, axis=0, keepdims=True)],
        )
        for k in range(1, n_peers):
            send(nsend.at[a], nrecv.at[a, k - 1], n_ids[a][k - 1], peer(k))

    def norm(a, out):
        total = nsend[a]
        for k in range(1, n_peers):
            frm = (lax.rem(sec + nsec - k // ntp, nsec), ctx, lax.rem(tp + ntp - k % ntp, ntp))
            arrive(nrecv.at[a, k - 1], n_ids[a][k - 1], frm)
            total = total + nrecv[a, k - 1]
        scale = lax.rsqrt(unpack_rows(total, 0, nsub) / full + EPS)
        slope = unpack_rows(total, nsub, nsub) / full
        o = ot[a]
        g = (scale * (lifted[a] - o * (scale * scale * slope))).astype(BF16)
        do[a, x] = g
        delta = jnp.sum(g.astype(F32) * o, axis=0, keepdims=True)
        pack_rows(dstat.at[a, x, nsub : 2 * nsub], [delta])
        send(do.at[a, x], do.at[a, x], do_ids[a][0], partner)
        send(dstat.at[a, x], dstat.at[a, x], do_ids[a][1], partner)
        out[...] = (gains[a] * (o * scale).T).astype(BF16)

    send_partial(SELF)
    self_forward(zoff(half), x)
    ring_arrive(mb, mb_ids, half, EARLY)
    for g in range(1, n_groups):
        cross_forward(g)
    combine(SELF)
    send_partial(CROSS)
    norm(SELF, self_out)
    combine(CROSS)

    def backward(a, h, keys, values, keys_t, slot, keep):
        dk = dv = None
        for t in range(rows // TQ):
            cols = slice(t * TQ, (t + 1) * TQ)
            q = qs[a, h, cols, :]
            g = do[a, h, :, cols]
            stat = dstat[a, h]
            lse = unpack_rows(stat, t * (TQ // 128), TQ // 128)
            delta = unpack_rows(stat, nsub + t * (TQ // 128), TQ // 128)
            s = dot(keys, q, 1, 1)
            if slot is not None:
                s = masked(s, slot, h, t * TQ)
            p = jnp.exp2(s * C2 - lse)
            ds = (p * (dot(values, g, 1, 0) - delta)).astype(BF16)
            dv_t = dot(p.astype(BF16), g, 1, 1)
            dk_t = dot(ds, q, 1, 0)
            dv = dv_t if dv is None else dv + dv_t
            dk = dk_t if dk is None else dk + dk_t
            dq[a, h, :, cols] = dq[a, h, :, cols] + dot(keys_t, ds, 1, 0)
        keep(0, dk * SCALE)
        keep(1, dv)

    def self_backward(offset, h, first):
        slot = lax.rem(z + offset, nz)

        def keep(j, value):
            kacc[offset, j] = value if first else kacc[offset, j] + value

        backward(SELF, h, kv[slot, 0], kv[slot, 1], kv[slot, 0].T, slot, keep)

    def back_blocks(count, start, step, first):
        def one(i, c):
            self_backward(lax.rem(start + i * step, nz), x if first else 1 - x, first)
            return c

        lax.fori_loop(0, count, one, 0)

    rs_ids, mrs_ids = ring_ids(), ring_ids()

    def reduce_step(dist, part, recv, snd, ids, pairs):
        for d, j in pairs:
            if (dist, d, j) in ids:
                own = part(d, j)
                if (dist + 1, d, j) in ids:
                    arrive(recv.at[d, dist, j], ids[dist + 1, d, j], neighbour[1 - d])
                    own = own + recv[d, dist, j].astype(F32)
                snd[d, dist - 1, j] = own.astype(BF16)
                send(snd.at[d, dist - 1, j], recv.at[d, dist - 1, j], ids[dist, d, j], neighbour[d])

    def do_arrive(a):
        arrive(do.at[a, 1 - x], do_ids[a][0], partner)
        arrive(dstat.at[a, 1 - x], do_ids[a][1], partner)

    def cross_backward(first):
        def one(g, c):
            def keep(j, value):
                at = pl.ds(g * per, per)
                value = value.reshape(per, srows, HEAD_DIM)
                ms[at, j] = value if first else ms[at, j] + value

            keys = cross_group(g, 0)
            backward(CROSS, x if first else 1 - x, keys, cross_group(g, 1), keys.T, None, keep)
            return c

        lax.fori_loop(0, n_groups, one, 0)

    def mem_step(dist):
        def part(d, j):
            return ms[((dist if d == 0 else nz - dist) + 1) % nz, j]

        reduce_step(dist, part, mrs_r, mrs_s, mrs_ids, LATE + EARLY)

    def self_step(dist, pairs):
        reduce_step(dist, lambda d, j: kacc[dist if d == 0 else nz - dist, j], rs_r, rs_s, rs_ids, pairs)

    def send_query(a):
        dqs[a] = dq[a, 1 - x].astype(BF16)
        send(dqs.at[a], dqr.at[a], dq_ids[a], partner)

    back_blocks(3, half - 1, 1, True)
    for dist in range(half - 2, 1, -1):
        back_blocks(2, dist, nz - 2 * dist, True)
    norm(CROSS, cross_out)
    do_arrive(SELF)
    back_blocks(1, half, 1, False)
    self_step(half, EARLY)
    back_blocks(2, half - 1, 2, False)
    self_step(half - 1, LATE)
    cross_backward(True)
    do_arrive(CROSS)
    cross_backward(False)
    mem_step(half)
    self_step(half - 1, EARLY)
    send_query(CROSS)
    for dist in range(half - 2, 1, -1):
        back_blocks(2, dist, nz - 2 * dist, False)
        mem_step(dist + 1)
        self_step(dist, LATE + EARLY)
    mem_step(2)
    back_blocks(3, nz - 1, 1, True)
    back_blocks(3, nz - 1, 1, False)
    send_query(SELF)
    mem_step(1)
    self_step(1, LATE + EARLY)

    def reduced(own, recv, ids, j):
        for d in range(2):
            arrive(recv.at[d, 0, j], ids[1, d, j], neighbour[1 - d])
            own = own + recv[d, 0, j].astype(F32)
        return own.astype(BF16)

    def finish_query(a, out):
        arrive(dqr.at[a], dq_ids[a], partner)
        out[...] = ((dq[a, x] + dqr[a].astype(F32)) * SCALE).T.astype(BF16)

    finish_query(CROSS, cross_query_grad)
    for j in range(2):
        mfin[j] = reduced(ms[1, j], mrs_r, mrs_ids, j)
    ret_ids = [sem_id() for _ in range(1, n_peers)]
    for k in range(1, n_peers):
        to = peer(k)
        src_rows = pl.ds(pl.multiple_of(to[0] * mrows, mrows), mrows)
        send(mfin.at[:, src_rows, :], mout.at[:, :, own_cols], ret_ids[k - 1], to)
    mine = pltpu.make_async_copy(mfin.at[:, own_rows, :], mout.at[:, :, own_cols], lsem.at[0])
    mine.start()
    finish_query(SELF, query_grad)
    mine.wait()
    key_grad[...] = reduced(kacc[0, 0], rs_r, rs_ids, 0)
    value_grad[...] = reduced(kacc[0, 1], rs_r, rs_ids, 1)
    for k in range(1, n_peers):
        fs, ft = lax.rem(sec + nsec - k // ntp, nsec), lax.rem(tp + ntp - k % ntp, ntp)
        cols = pl.ds(pl.multiple_of((fs * ntp + ft) * HEAD_DIM, HEAD_DIM), HEAD_DIM)
        arrive(mout.at[:, :, cols], ret_ids[k - 1], (fs, ctx, ft))
    mkey_grad[...] = mout[0]
    mvalue_grad[...] = mout[1]
    for c in sent:
        c.wait_send()


def write_out(*refs):
    sems = refs[-1]
    copies = [pltpu.make_async_copy(refs[i], refs[8 + i], sems.at[i]) for i in range(8)]
    for c in copies:
        c.start()
    for c in copies:
        c.wait()


def per_device(nz, nsec, ntp, *args):
    (sq, sk, sv, sgain, sgrad, cq, mk, mv, cgain, cgrad, bs) = args
    rows = sq.shape[0]
    mrows = mk.shape[0]
    half = nz // 2
    srows = nsec * mrows
    n_sems = 160
    hbm = pl.BlockSpec(memory_space=pltpu.HBM)
    vmem = pl.BlockSpec(memory_space=pltpu.VMEM)
    smem = pl.BlockSpec(memory_space=pltpu.SMEM)
    V = pltpu.VMEM
    frame, memory = V((rows, HEAD_DIM), BF16), V(mk.shape, BF16)
    results = pl.pallas_call(
        functools.partial(kernel, nz, nsec, ntp, n_sems),
        out_shape=(frame, frame, frame, frame, frame, frame, memory, memory),
        in_specs=[smem] + [hbm] * 10,
        out_specs=(vmem,) * 8,
        scratch_shapes=[
            V((nz, 2, rows, HEAD_DIM), BF16),
            V((2, 2, rows, HEAD_DIM), BF16),
            V((nz, 2, srows, HEAD_DIM), BF16),
            V((2, 2, HEAD_DIM, rows), F32),
            V((2, 2, 8, rows), F32),
            V((2, HEAD_DIM, rows), F32),
            V((2, HEAD_DIM, rows), F32),
            V((2, HEAD_DIM, rows), BF16),
            V((2, HEAD_DIM, rows), BF16),
            V((2, 8, 128), F32),
            V((2, 8, 128), F32),
            V((2, 8, 128), F32),
            V((2, nsec * ntp, 8, 128), F32),
            V((2, 2, HEAD_DIM, rows), BF16),
            V((2, 2, 8, 128), F32),
            V((2, 2, HEAD_DIM, rows), F32),
            V((2, HEAD_DIM, rows), BF16),
            V((2, HEAD_DIM, rows), BF16),
            V((nz, 2, rows, HEAD_DIM), F32),
            V((2, half, 2, rows, HEAD_DIM), BF16),
            V((2, half, 2, rows, HEAD_DIM), BF16),
            V((nz, 2, srows, HEAD_DIM), F32),
            V((2, half, 2, srows, HEAD_DIM), BF16),
            V((2, half, 2, srows, HEAD_DIM), BF16),
            V((2, srows, HEAD_DIM), BF16),
            V((2, mrows, nsec * ntp * HEAD_DIM), BF16),
            V((2, rows, HEAD_DIM), BF16),
            V((2, 1, HEAD_DIM), F32),
            pltpu.SemaphoreType.DMA((n_sems,)),
            pltpu.SemaphoreType.DMA((n_sems,)),
            pltpu.SemaphoreType.DMA((10,)),
        ],
        compiler_params=pltpu.CompilerParams(
            collective_id=0, has_side_effects=True, vmem_limit_bytes=56 * 1024 * 1024
        ),
        cost_estimate=pl.CostEstimate(flops=9_000_000_000, bytes_accessed=4_000_000, transcendentals=10_000_000),
    )(bs, sq, sk, sv, sgain.reshape(1, -1), sgrad, cq, mk, mv, cgain.reshape(1, -1), cgrad)
    return pl.pallas_call(
        write_out,
        out_shape=tuple(jax.ShapeDtypeStruct(r.shape, r.dtype) for r in results),
        in_specs=[vmem] * 8,
        out_specs=(pl.BlockSpec(memory_space=pl.ANY),) * 8,
        scratch_shapes=[pltpu.SemaphoreType.DMA((8,))],
        compiler_params=pltpu.CompilerParams(vmem_limit_bytes=32 * 1024 * 1024),
    )(*results)


def solution(mesh):
    nz, nsec, ntp = mesh.shape["ctx"] // 2, mesh.shape["sec"], mesh.shape["tp"]
    heads = ("sec", "tp")
    frame, gain, memory = P("ctx", heads), P(heads), P(("sec", "ctx"), None)
    return jax.shard_map(
        functools.partial(per_device, nz, nsec, ntp),
        mesh=mesh,
        in_specs=(frame, frame, frame, gain, frame, frame, memory, memory, gain, frame, P()),
        out_specs=(frame,) * 6 + (memory,) * 2,
        check_vma=False,
    )
```
